512 devices in a mesh: red: 64 (over z, y), rep: 8 (over x, core).
Axes of the slice: x: 4, y: 4, z: 16, core: 2. Of those that a mesh axis runs over, the one named last changes fastest.
Arguments:
- amplitudes: bfloat16 [7680, 960, 120], P(('rep', 'red')), may hold values from -6 to 6
- integrals: bfloat16 [960, 120, 8, 120], P('red', None, 'rep'), may hold values from -0.046875 to 0.046875
- other_terms: float32 [7680, 8, 120], P(('rep', 'red')), may hold values from -6 to 6
- occ_energy: float32 [120], replicated, may hold values from -2 to -0.5
- vir_energy: float32 [960], replicated, may hold values from 0.5 to 3
- occ_irrep: int32 [120], replicated, may hold values from 0 to 7, as said below
- vir_irrep: int32 [960], replicated, may hold values from 0 to 7, as said below
- slab_a: int32 [1], replicated, may hold values from 0 to 14
- slab_b: int32 [1], replicated, may hold values from 0 to 119
Outputs:
- new_amplitudes: float32 [7680, 8, 120], P(('rep', 'red'))
The draws below stay inside these ranges and needn't reach their ends.
Inputs may be any that keep to these rules, and one draw needn't show every extreme that they name: `occ_irrep`: labels are nondecreasing over the orbitals (orbitals ordered by irrep); the first is 0 and the last is 7. `vir_irrep`: labels are nondecreasing over the orbitals (orbitals ordered by irrep); the first is 0 and the last is 7.
All inputs are finite; a program needn't handle non-finite values.
Results may differ from the reference program's by a relative error of at most 0.0003.
Values may be sent and summed in bfloat16 or wider, within the bound.
No kernel may reach another device: no remote copies, remote signals or barrier semaphores. Data moves between devices by JAX's collectives and lax.ppermute only.
A program may use at most 64 MiB of HBM per device.

```python
import jax
import jax.numpy as jnp
from jax import lax

O = 120
V = 960
A = 64
B = 8


def sorted_labels(key, count):
    inner = jax.random.randint(key, (count - 2,), 0, 8).astype(jnp.int32)
    ends = jnp.array([0, 7], jnp.int32)
    return jnp.sort(jnp.concatenate([ends, inner]))


def draw_occ_irrep(key, part):
    key = jax.random.fold_in(key, 11)
    return sorted_labels(key, O)


def draw_vir_irrep(key, part):
    key = jax.random.fold_in(key, 23)
    return sorted_labels(key, V)


def block_scale(rng, extent, shards, least, top_value):
    def one(position, blocks):
        draws = jax.random.uniform(jax.random.fold_in(jax.random.fold_in(rng, 6), position), (blocks,), jnp.float32, least / len(shards), top_value / len(shards))
        return jnp.repeat(jnp.exp(draws), extent[position] // blocks).reshape((-1,) + (1,) * (len(extent) - position - 1))

    factor_of = one(*shards[0])
    for cut in shards[1:]:
        factor_of = factor_of * one(*cut)
    return factor_of


def noise(own_key, extent, deviation, limit, shards=(), held_as=jnp.bfloat16):
    loudness = block_scale(own_key, extent, shards, -0.22, 0.18) if shards else 1.0
    entries = jax.random.normal(own_key, extent, jnp.float32) * deviation * loudness
    return jnp.minimum(jnp.maximum(entries, -limit), limit).astype(held_as)


def setup_inputs(seed: int = 0) -> dict:
    streams_of = jax.random.split(jax.random.key(seed), 10)
    return {
        "amplitudes": noise(streams_of[0], (A * O, V, O), 1.0, 6.0, ((0, 512),)),
        "integrals": noise(streams_of[1], (V, O, B, O), (O * V // 8) ** -0.5, 0.046875, ((0, 64), (2, 8))),
        "other_terms": noise(streams_of[2], (A * O, B, O), 1.0, 6.0, ((0, 512),), jnp.float32),
        "occ_energy": jnp.clip(jax.random.uniform(streams_of[3], (O,), jnp.float32, -2.0, -0.5), -2.0, -0.5),
        "vir_energy": jnp.clip(jax.random.uniform(streams_of[4], (V,), jnp.float32, 0.5, 3.0), 0.5, 3.0),
        "occ_irrep": draw_occ_irrep(jax.random.fold_in(streams_of[9], 71), 0),
        "vir_irrep": draw_vir_irrep(jax.random.fold_in(streams_of[9], 71), 0),
        "slab_a": jax.random.randint(streams_of[7], (1,), 0, V // A).astype(jnp.int32),
        "slab_b": jax.random.randint(streams_of[8], (1,), 0, V // B).astype(jnp.int32),
    }


def pair_labels(left, right):
    return jnp.bitwise_xor(left[:, None], right[None, :])


def reference(amplitudes, integrals, other_terms, occ_energy, vir_energy, occ_irrep, vir_irrep, slab_a, slab_b):
    a_start = (slab_a[0] * A).astype(jnp.int32)
    b_start = (slab_b[0] * B).astype(jnp.int32)
    a_labels = lax.dynamic_slice_in_dim(vir_irrep, a_start, A)
    b_labels = lax.dynamic_slice_in_dim(vir_irrep, b_start, B)
    a_energy = lax.dynamic_slice_in_dim(vir_energy, a_start, A)
    b_energy = lax.dynamic_slice_in_dim(vir_energy, b_start, B)
    pair_ck = pair_labels(vir_irrep, occ_irrep)
    pair_bj = pair_labels(b_labels, occ_irrep)
    kept = (pair_ck[:, :, None, None] == pair_bj[None, None]).astype(jnp.bfloat16)
    kept_integrals = integrals * kept
    cycle_term = jnp.dot(amplitudes.reshape(A * O, V * O), kept_integrals.reshape(V * O, B * O),
                        preferred_element_type=jnp.float32).reshape(A * O, B, O)
    pair_ai = pair_labels(a_labels, occ_irrep).reshape(A * O)
    allowed = pair_ai[:, None, None] == pair_bj[None]
    row_energy = (occ_energy[None, :] - a_energy[:, None]).reshape(A * O)
    col_energy = occ_energy[None, :] - b_energy[:, None]
    denominator = row_energy[:, None, None] + col_energy[None]
    updated = (cycle_term + other_terms) / denominator
    return jnp.where(allowed, updated, jnp.zeros_like(updated))
```

```python
import functools

import jax
import jax.numpy as jnp
from jax import lax
from jax.experimental import pallas as pl
from jax.experimental.pallas import tpu as pltpu
from jax.sharding import Mesh, PartitionSpec as P

A = 64
B = 8
O = 120
V = 960
ROWS = 15
SLOTS = 24
GROUP = 5
PARTS = ROWS // GROUP
FAR = 4
NEAR = 16
REP = 8
LANES = 128
BF = jnp.bfloat16
F32 = jnp.float32


def pair_labels(left, right):
    return jnp.bitwise_xor(left[:, None], right[None, :])


def column_of(row):
    n = row.shape[1]
    same = lax.broadcasted_iota(jnp.int32, (n, n), 0) == lax.broadcasted_iota(jnp.int32, (n, n), 1)
    return jnp.sum(jnp.where(same, row.astype(F32), 0.0), axis=1, keepdims=True).astype(jnp.int32)


def positions(occ_row):
    n = occ_row.shape[1]
    occ_col = column_of(occ_row)
    k_col = lax.broadcasted_iota(jnp.int32, (n, n), 0)
    k_row = lax.broadcasted_iota(jnp.int32, (n, n), 1)
    same = occ_col == occ_row
    row = jnp.sum(jnp.where(same & (k_col < k_row), 1.0, 0.0), axis=0, keepdims=True)
    col = jnp.sum(jnp.where(same & (k_row < k_col), 1.0, 0.0), axis=1, keepdims=True)
    return occ_col, row.astype(jnp.int32), col.astype(jnp.int32)


def thirds(x):
    high = x.astype(BF)
    rest = x - high.astype(F32)
    middle = rest.astype(BF)
    low = (rest - middle.astype(F32)).astype(BF)
    return high, middle, low


def pack_integrals(place, vir_irrep, slab_b, occ_row, integrals, out, scratch):
    red, rep = place()
    occ = occ_row[...]
    occ_col, pos_row, _ = positions(occ)
    slot = lax.broadcasted_iota(jnp.int32, (SLOTS, O), 0)
    pick = jnp.where(slot == pos_row, 1.0, 0.0).astype(BF)
    b_label = vir_irrep[slab_b[0] * B + rep]
    scratch[...] = jnp.zeros_like(scratch)
    for c in range(ROWS):
        label = vir_irrep[red * ROWS + c] ^ b_label
        kept = jnp.where((occ_col ^ label) == occ, integrals[c].astype(F32), 0.0).astype(BF)
        first = LANES * (c // GROUP) + SLOTS * (c % GROUP)
        scratch[first : first + SLOTS, :O] = jnp.dot(pick, kept, preferred_element_type=F32)
    out[...] = scratch[...].astype(BF)


def pack_amplitudes(
    place, vir_irrep, occ_irrep, slab_a, occ_row, vir_rows, amplitudes, out, starts, chosen, row, packed
):
    red, rep = place()
    step = pl.program_id(0)
    occ = occ_row[...]

    @pl.when(step == 0)
    def _():
        _, _, pos_col = positions(occ)
        lane = lax.broadcasted_iota(jnp.int32, (O, LANES), 1)
        for u in range(GROUP):
            hit = (lane == pos_col + SLOTS * u) & (pos_col < SLOTS)
            chosen[u, :O] = jnp.where(hit, 1.0, 0.0).astype(BF)
        labels = vir_rows[...]
        for g in range(9):
            below = jnp.sum(jnp.where(labels < g, 1.0, 0.0), axis=1, keepdims=True)
            starts[g : g + 1] = jnp.broadcast_to(
                jnp.sum(below, axis=0, keepdims=True).astype(jnp.int32), (1, LANES)
            )
        packed[pl.ds(ROWS, V // GROUP, stride=16), :] = jnp.zeros((V // GROUP, LANES), F32)

    row_id = (rep * (FAR * NEAR) + red) * ROWS + step
    label = vir_irrep[slab_a[0] * A + row_id // O] ^ occ_irrep[row_id % O]
    partner = occ ^ label
    low = jnp.zeros((1, O), jnp.int32)
    high = jnp.zeros((1, O), jnp.int32)
    for g in range(8):
        low = jnp.where(partner == g, starts[g : g + 1, :O], low)
        high = jnp.where(partner == g, starts[g + 1 : g + 2, :O], high)
    c_index = lax.broadcasted_iota(jnp.int32, (V, O), 0)
    kept = (c_index >= low) & (c_index < high)
    row[:, :O] = jnp.where(kept, amplitudes[0].astype(F32), 0.0)
    total = jnp.zeros((V // GROUP, LANES), F32)
    for u in range(GROUP):
        part = row[pl.ds(u, V // GROUP, stride=GROUP), :]
        total += jnp.dot(part[:, :O].astype(BF), chosen[u, :O], preferred_element_type=F32)
    packed[pl.ds(step, V // GROUP, stride=16), :] = total

    @pl.when(step == ROWS - 1)
    def _():
        rows = PARTS * 16
        for e in range(NEAR):
            for far in range(FAR):
                first = (far * NEAR + e) * rows
                out[e, far * rows : (far + 1) * rows] = packed[first : first + rows].astype(BF)


def multiply(place, vir_irrep, slab_a, slab_b, occ_row, vir_rows, amps, ints, out, left):
    red, rep = place()
    far_own = red // NEAR
    occ = occ_row[...]
    _, _, pos_col = positions(occ)
    rows = NEAR * 16
    for s in range(NEAR):
        for block in range(FAR * PARTS):
            left[s * 16 : (s + 1) * 16, block * LANES : (block + 1) * LANES] = amps[
                s, block * 16 : (block + 1) * 16
            ]
    row = lax.broadcasted_iota(jnp.int32, (rows, 1), 0)
    local = (row // 16) * ROWS + row % 16
    second = local >= O
    i_index = jnp.where(second, local - O, local)
    i_label = jnp.zeros((rows, 1), jnp.int32)
    for g in range(1, 8):
        start = jnp.sum(jnp.where(occ < g, 1.0, 0.0), axis=1, keepdims=True).astype(jnp.int32)
        i_label += jnp.where(i_index >= start, 1, 0)
    a_first = slab_a[0] * A + (rep * FAR + far_own) * 2
    row_label = i_label ^ jnp.where(second, vir_irrep[a_first + 1], vir_irrep[a_first])
    lane = lax.broadcasted_iota(jnp.int32, (O, LANES), 1)
    main = jnp.zeros((rows, LANES), F32)
    rest = jnp.zeros((rows, LANES), F32)
    amounts = left[...]
    for pair in range(B // 2):
        right = jnp.concatenate([ints[2 * pair], ints[2 * pair + 1]], axis=1)
        both = jnp.dot(amounts, right, preferred_element_type=F32)
        for half in range(2):
            b = 2 * pair + half
            b_label = vir_irrep[slab_b[0] * B + b]
            part = both[:, half * LANES : half * LANES + O]
            part = jnp.where((row_label ^ b_label) == occ, part, 0.0)
            pieces = thirds(part)
            if SLOTS * b < LANES:
                pick = jnp.where(lane == pos_col + SLOTS * b, 1.0, 0.0).astype(BF)
                for piece in pieces:
                    main += jnp.dot(piece, pick, preferred_element_type=F32)
            if SLOTS * (b + 1) > LANES:
                pick = jnp.where(lane == pos_col + (SLOTS * b - LANES), 1.0, 0.0).astype(BF)
                for piece in pieces:
                    rest += jnp.dot(piece, pick, preferred_element_type=F32)
    moved = pltpu.roll(rest, LANES // 2, 1)
    for e in range(NEAR):
        out[e, :16] = main[e * 16 : (e + 1) * 16]
        out[e, 16:] = rest[e * 16 : e * 16 + 8] + moved[e * 16 + 8 : e * 16 + 16]


def finish(
    place, vir_irrep, occ_irrep, slab_a, slab_b, occ_energy, vir_energy, occ_row, energy_row, parts, other, out, cycle
):
    red, rep = place()
    occ = occ_row[...]
    _, pos_row, _ = positions(occ)
    total = parts[0]
    for s in range(1, NEAR):
        total += parts[s]
    main = total[:16]
    rest = jnp.concatenate([total[16:], pltpu.roll(total[16:], LANES // 2, 1)], axis=0)
    mains = jnp.concatenate(thirds(main), axis=0)
    rests = jnp.concatenate(thirds(rest), axis=0)
    lane = lax.broadcasted_iota(jnp.int32, (LANES, O), 0)
    for b in range(B):
        value = jnp.zeros((48, O), F32)
        if SLOTS * b < LANES:
            pick = jnp.where(lane == pos_row + SLOTS * b, 1.0, 0.0).astype(BF)
            value += jnp.dot(mains, pick, preferred_element_type=F32)
        if SLOTS * (b + 1) > LANES:
            at = pos_row + (SLOTS * b - LANES)
            pick = jnp.where((lane == at) & (lane < LANES // 2), 1.0, 0.0).astype(BF)
            value += jnp.dot(rests, pick, preferred_element_type=F32)
        cycle[pl.ds(b, 16, stride=B), :O] = (value[:16] + value[16:32]) + value[32:]
    b_first = slab_b[0] * B
    b_index = lax.broadcasted_iota(jnp.int32, (B, 1), 0)
    b_label = jnp.zeros((B, 1), jnp.int32)
    b_energy = jnp.zeros((B, 1), F32)
    for b in range(B):
        b_label = jnp.where(b_index == b, vir_irrep[b_first + b], b_label)
        b_energy = jnp.where(b_index == b, vir_energy[b_first + b], b_energy)
    pair_bj = b_label ^ occ
    col_energy = energy_row[...] - b_energy
    for r in range(ROWS):
        row_id = (rep * (FAR * NEAR) + red) * ROWS + r
        a = slab_a[0] * A + row_id // O
        i = row_id % O
        label = vir_irrep[a] ^ occ_irrep[i]
        row_energy = occ_energy[i] - vir_energy[a]
        updated = (cycle[r * B : (r + 1) * B, :O] + other[r]) / (row_energy + col_energy)
        out[r] = jnp.where(pair_bj == label, updated, 0.0)


def own_place():
    return lax.axis_index("far") * NEAR + lax.axis_index("near"), lax.axis_index("rep")


SMEM = pl.BlockSpec(memory_space=pltpu.SMEM)
VMEM = pl.BlockSpec(memory_space=pltpu.VMEM)


def params(limit):
    return pltpu.CompilerParams(vmem_limit_bytes=limit * 1024 * 1024)


def call_pack_integrals(place, vir_irrep, slab_b, occ_row, integrals, **kw):
    return pl.pallas_call(
        functools.partial(pack_integrals, place),
        out_shape=jax.ShapeDtypeStruct((PARTS * LANES, LANES), BF),
        in_specs=[SMEM, SMEM, VMEM, VMEM],
        out_specs=VMEM,
        scratch_shapes=[pltpu.VMEM((PARTS * LANES, LANES), F32)],
        compiler_params=params(16),
        cost_estimate=pl.CostEstimate(flops=2 * 10**7, bytes_accessed=600000, transcendentals=0),
        name="pack_integrals",
        **kw,
    )(vir_irrep, slab_b, occ_row, integrals)


def call_pack_amplitudes(place, vir_irrep, occ_irrep, slab_a, occ_row, vir_rows, amplitudes, **kw):
    fixed = lambda shape: pl.BlockSpec(shape, lambda r: (0,) * len(shape))
    return pl.pallas_call(
        functools.partial(pack_amplitudes, place),
        out_shape=jax.ShapeDtypeStruct((NEAR, FAR * PARTS * 16, LANES), BF),
        grid=(ROWS,),
        in_specs=[SMEM, SMEM, SMEM, fixed((1, O)), fixed((B, O)), pl.BlockSpec((1, V, O), lambda r: (r, 0, 0))],
        out_specs=fixed((NEAR, FAR * PARTS * 16, LANES)),
        scratch_shapes=[
            pltpu.VMEM((16, LANES), jnp.int32),
            pltpu.VMEM((GROUP, LANES, LANES), BF),
            pltpu.VMEM((V, LANES), F32),
            pltpu.VMEM((V // GROUP * 16, LANES), F32),
        ],
        compiler_params=params(32),
        cost_estimate=pl.CostEstimate(flops=10**9, bytes_accessed=4500000, transcendentals=0),
        name="pack_amplitudes",
        **kw,
    )(vir_irrep, occ_irrep, slab_a, occ_row, vir_rows, amplitudes)


def call_multiply(place, vir_irrep, slab_a, slab_b, occ_row, vir_rows, amps, ints, **kw):
    return pl.pallas_call(
        functools.partial(multiply, place),
        out_shape=jax.ShapeDtypeStruct((NEAR, 24, LANES), F32),
        in_specs=[SMEM, SMEM, SMEM, VMEM, VMEM, VMEM, VMEM],
        out_specs=VMEM,
        scratch_shapes=[pltpu.VMEM((NEAR * 16, FAR * PARTS * LANES), BF)],
        compiler_params=params(48),
        name="multiply",
        **kw,
    )(vir_irrep, slab_a, slab_b, occ_row, vir_rows, amps, ints)


def call_finish(place, vir_irrep, occ_irrep, slab_a, slab_b, occ_energy, vir_energy, occ_row, energy_row, parts, other, **kw):
    return pl.pallas_call(
        functools.partial(finish, place),
        out_shape=jax.ShapeDtypeStruct((ROWS, B, O), F32),
        in_specs=[SMEM] * 6 + [VMEM] * 4,
        out_specs=VMEM,
        scratch_shapes=[pltpu.VMEM((16 * B, LANES), F32)],
        compiler_params=params(16),
        name="finish",
        **kw,
    )(vir_irrep, occ_irrep, slab_a, slab_b, occ_energy, vir_energy, occ_row, energy_row, parts, other)


def packed_form(amplitudes, integrals, other_terms, occ_energy, vir_energy, occ_irrep, vir_irrep, slab_a, slab_b):
    occ_row = occ_irrep.reshape(1, O)
    vir_rows = vir_irrep.reshape(B, O)
    ints = call_pack_integrals(own_place, vir_irrep, slab_b, occ_row, integrals.reshape(ROWS, O, O))
    ints = lax.all_gather(ints, "far", axis=0, tiled=True)
    ints = lax.all_gather(ints, "rep", axis=0)
    amps = call_pack_amplitudes(own_place, vir_irrep, occ_irrep, slab_a, occ_row, vir_rows, amplitudes)
    amps = lax.all_to_all(amps, "near", 0, 0, tiled=True)
    parts = call_multiply(own_place, vir_irrep, slab_a, slab_b, occ_row, vir_rows, amps, ints)
    parts = lax.all_to_all(parts, "near", 0, 0, tiled=True)
    return call_finish(
        own_place, vir_irrep, occ_irrep, slab_a, slab_b, occ_energy, vir_energy,
        occ_row, occ_energy.reshape(1, O), parts, other_terms,
    )


def whole_form(amplitudes, integrals, other_terms, occ_energy, vir_energy, occ_irrep, vir_irrep, slab_a, slab_b):
    red = ("far", "near")
    red_count = FAR * NEAR
    rows_dev = amplitudes.shape[0]
    vir_local = integrals.shape[0]
    b_local = integrals.shape[2]
    occupied = occ_energy.shape[0]
    a_start = slab_a[0] * A
    b_start = slab_b[0] * B
    b_labels = lax.dynamic_slice_in_dim(vir_irrep, b_start, B)
    b_energy = lax.dynamic_slice_in_dim(vir_energy, b_start, B)
    c_labels = lax.dynamic_slice_in_dim(vir_irrep, lax.axis_index(red) * vir_local, vir_local)
    pair_ck = pair_labels(c_labels, occ_irrep)
    pair_bj = pair_labels(b_labels, occ_irrep)
    own_pairs = lax.dynamic_slice_in_dim(pair_bj, lax.axis_index("rep") * b_local, b_local, 0)
    local_kept = (pair_ck[:, :, None, None] == own_pairs[None, None]).astype(jnp.bfloat16)
    gathered = lax.all_gather(integrals * local_kept, "rep", axis=2, tiled=True)
    exchanged = lax.all_to_all(amplitudes, red, split_axis=1, concat_axis=0, tiled=True)
    flat_amps = exchanged.reshape(exchanged.shape[0], vir_local * occupied)
    flat_ints = gathered.reshape(vir_local * occupied, B * occupied)
    mine = lax.psum_scatter(
        jnp.dot(flat_amps, flat_ints, preferred_element_type=jnp.float32),
        red,
        scatter_dimension=0,
        tiled=True,
    )
    cycle_term = mine.reshape(rows_dev, B, occupied)
    first_global = (lax.axis_index("rep") * red_count + lax.axis_index(red)) * rows_dev
    row_ids = first_global + jnp.arange(rows_dev, dtype=jnp.int32)
    a_index = a_start + row_ids // occupied
    i_index = row_ids % occupied
    pair_ai = jnp.bitwise_xor(vir_irrep[a_index], occ_irrep[i_index])
    allowed = pair_ai[:, None, None] == pair_bj[None]
    row_energy = occ_energy[i_index] - vir_energy[a_index]
    col_energy = occ_energy[None, :] - b_energy[:, None]
    denominator = row_energy[:, None, None] + col_energy[None]
    updated = (cycle_term + other_terms) / denominator
    return jnp.where(allowed, updated, jnp.zeros_like(updated))


def on_device(*args):
    occ_irrep = args[5]
    crowded = jnp.any(occ_irrep[SLOTS:] == occ_irrep[:-SLOTS])
    return lax.cond(crowded, whole_form, packed_form, *args)


def solution(mesh):
    split = Mesh(mesh.devices.reshape(FAR, NEAR, REP), ("far", "near", "rep"))
    placed = (
        P(("rep", "far", "near"), None, None),
        P(("far", "near"), None, "rep", None),
        P(("rep", "far", "near"), None, None),
        P(),
        P(),
        P(),
        P(),
        P(),
        P(),
    )
    return jax.shard_map(
        on_device,
        mesh=split,
        in_specs=placed,
        out_specs=P(("rep", "far", "near"), None, None),
        check_vma=False,
    )
```

```python
import functools

import jax
import jax.numpy as jnp
from jax import lax
from jax.experimental import pallas as pl
from jax.experimental.pallas import tpu as pltpu
from jax.sharding import Mesh, PartitionSpec as P

A = 64
B = 8
O = 120
V = 960
ROWS = 15
SLOTS = 24
GROUP = 5
PARTS = ROWS // GROUP
STEP = 5
FAR = 4
NEAR = 16
REP = 8
LANES = 128
BF = jnp.bfloat16
F32 = jnp.float32


def pair_labels(left, right):
    return jnp.bitwise_xor(left[:, None], right[None, :])


def column_of(row):
    n = row.shape[1]
    same = lax.broadcasted_iota(jnp.int32, (n, n), 0) == lax.broadcasted_iota(jnp.int32, (n, n), 1)
    return jnp.sum(jnp.where(same, row.astype(F32), 0.0), axis=1, keepdims=True).astype(jnp.int32)


def positions(occ_row):
    n = occ_row.shape[1]
    occ_col = column_of(occ_row)
    k_col = lax.broadcasted_iota(jnp.int32, (n, n), 0)
    k_row = lax.broadcasted_iota(jnp.int32, (n, n), 1)
    same = occ_col == occ_row
    row = jnp.sum(jnp.where(same & (k_col < k_row), 1.0, 0.0), axis=0, keepdims=True)
    col = jnp.sum(jnp.where(same & (k_row < k_col), 1.0, 0.0), axis=1, keepdims=True)
    return occ_col, row.astype(jnp.int32), col.astype(jnp.int32)


def thirds(x):
    high = x.astype(BF)
    rest = x - high.astype(F32)
    middle = rest.astype(BF)
    low = (rest - middle.astype(F32)).astype(BF)
    return high, middle, low


def pack_integrals(place, vir_irrep, slab_b, occ_row, integrals, out, scratch):
    red, rep = place()
    occ = occ_row[...]
    occ_col, pos_row, _ = positions(occ)
    slot = lax.broadcasted_iota(jnp.int32, (SLOTS, O), 0)
    pick = jnp.where(slot == pos_row, 1.0, 0.0).astype(BF)
    b_label = vir_irrep[slab_b[0] * B + rep]
    scratch[...] = jnp.zeros_like(scratch)
    for c in range(ROWS):
        label = vir_irrep[red * ROWS + c] ^ b_label
        kept = jnp.where((occ_col ^ label) == occ, integrals[c].astype(F32), 0.0).astype(BF)
        first = LANES * (c // GROUP) + SLOTS * (c % GROUP)
        scratch[first : first + SLOTS, :O] = jnp.dot(pick, kept, preferred_element_type=F32)
    out[...] = scratch[...].astype(BF)


def pack_amplitudes(
    place, vir_irrep, occ_irrep, slab_a, occ_row, vir_rows, amplitudes, out, most, starts, chosen, row, packed
):
    red, rep = place()
    step = pl.program_id(0)
    occ = occ_row[...]

    @pl.when(step == 0)
    def _():
        _, pos_row, pos_col = positions(occ)
        most[0, 0] = jnp.max(pos_row)
        lane = lax.broadcasted_iota(jnp.int32, (O, LANES), 1)
        chosen[...] = jnp.zeros_like(chosen)
        for u in range(GROUP):
            hit = (lane == pos_col + SLOTS * u) & (pos_col < SLOTS)
            chosen[u * LANES : u * LANES + O] = jnp.where(hit, 1.0, 0.0).astype(BF)
        labels = vir_rows[...]
        for g in range(9):
            below = jnp.sum(jnp.where(labels < g, 1.0, 0.0), axis=1, keepdims=True)
            starts[g : g + 1] = jnp.broadcast_to(
                jnp.sum(below, axis=0, keepdims=True).astype(jnp.int32), (1, LANES)
            )
        packed[pl.ds(ROWS, V // GROUP, stride=16), :] = jnp.zeros((V // GROUP, LANES), F32)
        row[...] = jnp.zeros_like(row)

    for j in range(STEP):
        row_id = (rep * (FAR * NEAR) + red) * ROWS + step * STEP + j
        label = vir_irrep[slab_a[0] * A + row_id // O] ^ occ_irrep[row_id % O]
        partner = occ ^ label
        low = jnp.zeros((1, O), jnp.int32)
        high = jnp.zeros((1, O), jnp.int32)
        for g in range(8):
            low = jnp.where(partner == g, starts[g : g + 1, :O], low)
            high = jnp.where(partner == g, starts[g + 1 : g + 2, :O], high)
        c_index = lax.broadcasted_iota(jnp.int32, (V, O), 0)
        kept = (c_index >= low) & (c_index < high)
        row[j, :, :O] = jnp.where(kept, amplitudes[j].astype(F32), 0.0)
    for j in range(STEP):
        left = jnp.concatenate(
            [row[j, pl.ds(u, V // GROUP, stride=GROUP), :].astype(BF) for u in range(GROUP)], axis=1
        )
        total = jnp.dot(left, chosen[...], preferred_element_type=F32)
        packed[pl.ds(step * STEP + j, V // GROUP, stride=16), :] = total

    @pl.when(step == ROWS // STEP - 1)
    def _():
        rows = PARTS * 16
        for e in range(NEAR):
            for far in range(FAR):
                first = (far * NEAR + e) * rows
                out[e, far * rows : (far + 1) * rows] = packed[first : first + rows].astype(BF)


def multiply(place, vir_irrep, slab_a, slab_b, occ_row, amps, ints, out, left, row_label, total):
    red, rep = place()
    step = pl.program_id(0)
    occ = occ_row[...]
    rows = NEAR * 16

    @pl.when(step == 0)
    def _():
        for s in range(NEAR):
            for block in range(FAR * PARTS):
                left[s * 16 : (s + 1) * 16, block * LANES : (block + 1) * LANES] = amps[
                    s, block * 16 : (block + 1) * 16
                ]
        row = lax.broadcasted_iota(jnp.int32, (rows, LANES), 0)
        local = (row // 16) * ROWS + row % 16
        second = local >= O
        i_index = jnp.where(second, local - O, local)
        i_label = jnp.zeros((rows, LANES), jnp.int32)
        for g in range(1, 8):
            start = jnp.sum(jnp.where(occ < g, 1.0, 0.0), axis=1, keepdims=True).astype(jnp.int32)
            i_label += jnp.where(i_index >= start, 1, 0)
        a_first = slab_a[0] * A + (rep * FAR + red // NEAR) * 2
        row_label[...] = i_label ^ jnp.where(second, vir_irrep[a_first + 1], vir_irrep[a_first])
        total[...] = jnp.zeros_like(total)

    _, _, pos_col = positions(occ)
    pad = jnp.full((1, LANES - O), 64, jnp.int32)
    occ_lanes = jnp.concatenate([occ, pad], axis=1)
    lane = lax.broadcasted_iota(jnp.int32, (O, 2 * LANES), 1)
    right = jnp.concatenate([ints[0], ints[1]], axis=1)
    both = jnp.dot(left[...], right, preferred_element_type=F32)
    for half in range(2):
        b = 2 * step + half
        b_label = vir_irrep[slab_b[0] * B + b]
        part = both[:, half * LANES : (half + 1) * LANES]
        part = jnp.where((row_label[...] ^ b_label) == occ_lanes, part, 0.0)
        pick = jnp.where(lane == pos_col + SLOTS * b, 1.0, 0.0)
        pick = jnp.concatenate([pick, jnp.zeros((LANES - O, 2 * LANES), F32)], axis=0).astype(BF)
        total[...] += jnp.dot(
            jnp.concatenate(thirds(part), axis=1),
            jnp.concatenate([pick] * 3, axis=0),
            preferred_element_type=F32,
        )

    @pl.when(step == B // 2 - 1)
    def _():
        rest = total[:, LANES:]
        moved = pltpu.roll(rest, LANES // 2, 1)
        for e in range(NEAR):
            out[e, :16] = total[e * 16 : (e + 1) * 16, :LANES]
            out[e, 16:] = rest[e * 16 : e * 16 + 8] + moved[e * 16 + 8 : e * 16 + 16]


def finish(
    place, vir_irrep, occ_irrep, slab_a, slab_b, occ_energy, vir_energy, occ_row, energy_row, parts, other, out, cycle
):
    red, rep = place()
    occ = occ_row[...]
    _, pos_row, _ = positions(occ)
    total = parts[0]
    for s in range(1, NEAR):
        total += parts[s]
    main = total[:16]
    rest = jnp.concatenate([total[16:], pltpu.roll(total[16:], LANES // 2, 1)], axis=0)
    mains = jnp.concatenate(thirds(main), axis=0)
    rests = jnp.concatenate(thirds(rest), axis=0)
    lane = lax.broadcasted_iota(jnp.int32, (LANES, O), 0)
    for b in range(B):
        value = jnp.zeros((48, O), F32)
        if SLOTS * b < LANES:
            pick = jnp.where(lane == pos_row + SLOTS * b, 1.0, 0.0).astype(BF)
            value += jnp.dot(mains, pick, preferred_element_type=F32)
        if SLOTS * (b + 1) > LANES:
            at = pos_row + (SLOTS * b - LANES)
            pick = jnp.where((lane == at) & (lane < LANES // 2), 1.0, 0.0).astype(BF)
            value += jnp.dot(rests, pick, preferred_element_type=F32)
        cycle[pl.ds(b, 16, stride=B), :O] = (value[:16] + value[16:32]) + value[32:]
    b_first = slab_b[0] * B
    b_index = lax.broadcasted_iota(jnp.int32, (B, 1), 0)
    b_label = jnp.zeros((B, 1), jnp.int32)
    b_energy = jnp.zeros((B, 1), F32)
    for b in range(B):
        b_label = jnp.where(b_index == b, vir_irrep[b_first + b], b_label)
        b_energy = jnp.where(b_index == b, vir_energy[b_first + b], b_energy)
    pair_bj = b_label ^ occ
    col_energy = energy_row[...] - b_energy
    for r in range(ROWS):
        row_id = (rep * (FAR * NEAR) + red) * ROWS + r
        a = slab_a[0] * A + row_id // O
        i = row_id % O
        label = vir_irrep[a] ^ occ_irrep[i]
        row_energy = occ_energy[i] - vir_energy[a]
        updated = (cycle[r * B : (r + 1) * B, :O] + other[r]) / (row_energy + col_energy)
        out[r] = jnp.where(pair_bj == label, updated, 0.0)


def own_place():
    return lax.axis_index("far") * NEAR + lax.axis_index("near"), lax.axis_index("rep")


SMEM = pl.BlockSpec(memory_space=pltpu.SMEM)
VMEM = pl.BlockSpec(memory_space=pltpu.VMEM)


def params(limit):
    return pltpu.CompilerParams(vmem_limit_bytes=limit * 1024 * 1024)


def call_pack_integrals(place, vir_irrep, slab_b, occ_row, integrals, **kw):
    return pl.pallas_call(
        functools.partial(pack_integrals, place),
        out_shape=jax.ShapeDtypeStruct((PARTS * LANES, LANES), BF),
        in_specs=[SMEM, SMEM, VMEM, VMEM],
        out_specs=VMEM,
        scratch_shapes=[pltpu.VMEM((PARTS * LANES, LANES), F32)],
        compiler_params=params(16),
        cost_estimate=pl.CostEstimate(flops=2 * 10**7, bytes_accessed=600000, transcendentals=0),
        name="pack_integrals",
        **kw,
    )(vir_irrep, slab_b, occ_row, integrals)


def fixed(shape):
    return pl.BlockSpec(shape, lambda step: (0,) * len(shape))


def call_pack_amplitudes(place, vir_irrep, occ_irrep, slab_a, occ_row, vir_rows, amplitudes, **kw):
    return pl.pallas_call(
        functools.partial(pack_amplitudes, place),
        out_shape=(
            jax.ShapeDtypeStruct((NEAR, FAR * PARTS * 16, LANES), BF),
            jax.ShapeDtypeStruct((1, 1), jnp.int32),
        ),
        grid=(ROWS // STEP,),
        in_specs=[SMEM, SMEM, SMEM, fixed((1, O)), fixed((B, O)), pl.BlockSpec((STEP, V, O), lambda r: (r, 0, 0))],
        out_specs=(fixed((NEAR, FAR * PARTS * 16, LANES)), SMEM),
        scratch_shapes=[
            pltpu.VMEM((16, LANES), jnp.int32),
            pltpu.VMEM((GROUP * LANES, LANES), BF),
            pltpu.VMEM((STEP, V, LANES), F32),
            pltpu.VMEM((V // GROUP * 16, LANES), F32),
        ],
        compiler_params=params(32),
        cost_estimate=pl.CostEstimate(flops=10**9, bytes_accessed=4500000, transcendentals=0),
        name="pack_amplitudes",
        **kw,
    )(vir_irrep, occ_irrep, slab_a, occ_row, vir_rows, amplitudes)


def call_multiply(place, vir_irrep, slab_a, slab_b, occ_row, amps, ints, **kw):
    depth = FAR * PARTS * LANES
    return pl.pallas_call(
        functools.partial(multiply, place),
        out_shape=jax.ShapeDtypeStruct((NEAR, 24, LANES), F32),
        grid=(B // 2,),
        in_specs=[
            SMEM, SMEM, SMEM, fixed((1, O)), fixed((NEAR, FAR * PARTS * 16, LANES)),
            pl.BlockSpec((2, depth, LANES), lambda step: (step, 0, 0)),
        ],
        out_specs=fixed((NEAR, 24, LANES)),
        scratch_shapes=[
            pltpu.VMEM((NEAR * 16, depth), BF),
            pltpu.VMEM((NEAR * 16, LANES), jnp.int32),
            pltpu.VMEM((NEAR * 16, 2 * LANES), F32),
        ],
        compiler_params=params(60),
        name="multiply",
        **kw,
    )(vir_irrep, slab_a, slab_b, occ_row, amps, ints)


def call_finish(place, vir_irrep, occ_irrep, slab_a, slab_b, occ_energy, vir_energy, occ_row, energy_row, parts, other, **kw):
    return pl.pallas_call(
        functools.partial(finish, place),
        out_shape=jax.ShapeDtypeStruct((ROWS, B, O), F32),
        in_specs=[SMEM] * 6 + [VMEM] * 4,
        out_specs=VMEM,
        scratch_shapes=[pltpu.VMEM((16 * B, LANES), F32)],
        compiler_params=params(16),
        name="finish",
        **kw,
    )(vir_irrep, occ_irrep, slab_a, slab_b, occ_energy, vir_energy, occ_row, energy_row, parts, other)


def whole_form(amplitudes, integrals, other_terms, occ_energy, vir_energy, occ_irrep, vir_irrep, slab_a, slab_b):
    red = ("far", "near")
    red_count = FAR * NEAR
    rows_dev = amplitudes.shape[0]
    vir_local = integrals.shape[0]
    b_local = integrals.shape[2]
    occupied = occ_energy.shape[0]
    a_start = slab_a[0] * A
    b_start = slab_b[0] * B
    b_labels = lax.dynamic_slice_in_dim(vir_irrep, b_start, B)
    b_energy = lax.dynamic_slice_in_dim(vir_energy, b_start, B)
    c_labels = lax.dynamic_slice_in_dim(vir_irrep, lax.axis_index(red) * vir_local, vir_local)
    pair_ck = pair_labels(c_labels, occ_irrep)
    pair_bj = pair_labels(b_labels, occ_irrep)
    own_pairs = lax.dynamic_slice_in_dim(pair_bj, lax.axis_index("rep") * b_local, b_local, 0)
    local_kept = (pair_ck[:, :, None, None] == own_pairs[None, None]).astype(jnp.bfloat16)
    gathered = lax.all_gather(integrals * local_kept, "rep", axis=2, tiled=True)
    exchanged = lax.all_to_all(amplitudes, red, split_axis=1, concat_axis=0, tiled=True)
    flat_amps = exchanged.reshape(exchanged.shape[0], vir_local * occupied)
    flat_ints = gathered.reshape(vir_local * occupied, B * occupied)
    mine = lax.psum_scatter(
        jnp.dot(flat_amps, flat_ints, preferred_element_type=jnp.float32),
        red,
        scatter_dimension=0,
        tiled=True,
    )
    cycle_term = mine.reshape(rows_dev, B, occupied)
    first_global = (lax.axis_index("rep") * red_count + lax.axis_index(red)) * rows_dev
    row_ids = first_global + jnp.arange(rows_dev, dtype=jnp.int32)
    a_index = a_start + row_ids // occupied
    i_index = row_ids % occupied
    pair_ai = jnp.bitwise_xor(vir_irrep[a_index], occ_irrep[i_index])
    allowed = pair_ai[:, None, None] == pair_bj[None]
    row_energy = occ_energy[i_index] - vir_energy[a_index]
    col_energy = occ_energy[None, :] - b_energy[:, None]
    denominator = row_energy[:, None, None] + col_energy[None]
    updated = (cycle_term + other_terms) / denominator
    return jnp.where(allowed, updated, jnp.zeros_like(updated))


def on_device(
    amplitudes, integrals, other_terms, occ_energy, vir_energy, occ_irrep, vir_irrep, slab_a, slab_b
):
    occ_row = occ_irrep.reshape(1, O)
    vir_rows = vir_irrep.reshape(B, O)
    ints = call_pack_integrals(own_place, vir_irrep, slab_b, occ_row, integrals.reshape(ROWS, O, O))
    ints = lax.all_gather(ints, "far", axis=0, tiled=True)
    ints = lax.all_gather(ints, "rep", axis=0)
    amps, most = call_pack_amplitudes(own_place, vir_irrep, occ_irrep, slab_a, occ_row, vir_rows, amplitudes)
    amps = lax.all_to_all(amps, "near", 0, 0, tiled=True)
    parts = call_multiply(own_place, vir_irrep, slab_a, slab_b, occ_row, amps, ints)
    parts = lax.all_to_all(parts, "near", 0, 0, tiled=True)

    def packed_form(amplitudes, integrals, *rest):
        other_terms, occ_energy, vir_energy, occ_irrep, vir_irrep, slab_a, slab_b, parts = rest
        return call_finish(
            own_place, vir_irrep, occ_irrep, slab_a, slab_b, occ_energy, vir_energy,
            occ_irrep.reshape(1, O), occ_energy.reshape(1, O), parts, other_terms,
        )

    return lax.cond(
        most[0, 0] >= SLOTS, lambda *args: whole_form(*args[:-1]), packed_form,
        amplitudes, integrals, other_terms, occ_energy, vir_energy, occ_irrep, vir_irrep, slab_a, slab_b, parts,
    )


def solution(mesh):
    split = Mesh(mesh.devices.reshape(FAR, NEAR, REP), ("far", "near", "rep"))
    placed = (
        P(("rep", "far", "near"), None, None),
        P(("far", "near"), None, "rep", None),
        P(("rep", "far", "near"), None, None),
        P(),
        P(),
        P(),
        P(),
        P(),
        P(),
    )
    return jax.shard_map(
        on_device,
        mesh=split,
        in_specs=placed,
        out_specs=P(("rep", "far", "near"), None, None),
        check_vma=False,
    )
```

```python
import functools

import jax
import jax.numpy as jnp
from jax import lax
from jax.experimental import pallas as pl
from jax.experimental.pallas import tpu as pltpu
from jax.sharding import Mesh, PartitionSpec as P

A = 64
B = 8
O = 120
V = 960
ROWS = 15
SLOTS = 24
GROUP = 5
PARTS = ROWS // GROUP
STEP = 5
FAR = 4
NEAR = 16
REP = 8
LANES = 128
BF = jnp.bfloat16
F32 = jnp.float32


def pair_labels(left, right):
    return jnp.bitwise_xor(left[:, None], right[None, :])


def column_of(row):
    n = row.shape[1]
    same = lax.broadcasted_iota(jnp.int32, (n, n), 0) == lax.broadcasted_iota(jnp.int32, (n, n), 1)
    return jnp.sum(jnp.where(same, row.astype(F32), 0.0), axis=1, keepdims=True).astype(jnp.int32)


def positions(occ_row):
    n = occ_row.shape[1]
    occ_col = column_of(occ_row)
    k_col = lax.broadcasted_iota(jnp.int32, (n, n), 0)
    k_row = lax.broadcasted_iota(jnp.int32, (n, n), 1)
    same = occ_col == occ_row
    row = jnp.sum(jnp.where(same & (k_col < k_row), 1.0, 0.0), axis=0, keepdims=True)
    col = jnp.sum(jnp.where(same & (k_row < k_col), 1.0, 0.0), axis=1, keepdims=True)
    return occ_col, row.astype(jnp.int32), col.astype(jnp.int32)


def thirds(x):
    high = x.astype(BF)
    rest = x - high.astype(F32)
    middle = rest.astype(BF)
    low = (rest - middle.astype(F32)).astype(BF)
    return high, middle, low


def pack_integrals(place, vir_irrep, slab_b, occ_row, integrals, out, scratch):
    red, rep = place()
    occ = occ_row[...]
    occ_col, pos_row, _ = positions(occ)
    slot = lax.broadcasted_iota(jnp.int32, (SLOTS, O), 0)
    pick = jnp.where(slot == pos_row, 1.0, 0.0).astype(BF)
    b_label = vir_irrep[slab_b[0] * B + rep]
    scratch[...] = jnp.zeros_like(scratch)
    for c in range(ROWS):
        label = vir_irrep[red * ROWS + c] ^ b_label
        kept = jnp.where((occ_col ^ label) == occ, integrals[c].astype(F32), 0.0).astype(BF)
        first = LANES * (c // GROUP) + SLOTS * (c % GROUP)
        scratch[first : first + SLOTS, :O] = jnp.dot(pick, kept, preferred_element_type=F32)
    packed = scratch[...].astype(BF)
    for far in range(FAR):
        out[far] = packed


def pack_amplitudes(
    place, vir_irrep, occ_irrep, slab_a, occ_row, vir_rows, amplitudes, out, most, starts, chosen, row, packed
):
    red, rep = place()
    step = pl.program_id(0)
    occ = occ_row[...]

    @pl.when(step == 0)
    def _():
        _, pos_row, pos_col = positions(occ)
        most[0, 0] = jnp.max(pos_row)
        lane = lax.broadcasted_iota(jnp.int32, (O, LANES), 1)
        chosen[...] = jnp.zeros_like(chosen)
        for u in range(GROUP):
            hit = (lane == pos_col + SLOTS * u) & (pos_col < SLOTS)
            chosen[u * LANES : u * LANES + O] = jnp.where(hit, 1.0, 0.0).astype(BF)
        labels = vir_rows[...]
        for g in range(9):
            below = jnp.sum(jnp.where(labels < g, 1.0, 0.0), axis=1, keepdims=True)
            starts[g : g + 1] = jnp.broadcast_to(
                jnp.sum(below, axis=0, keepdims=True).astype(jnp.int32), (1, LANES)
            )
        packed[pl.ds(ROWS, V // GROUP, stride=16), :] = jnp.zeros((V // GROUP, LANES), F32)
        row[...] = jnp.zeros_like(row)

    for j in range(STEP):
        row_id = (rep * (FAR * NEAR) + red) * ROWS + step * STEP + j
        label = vir_irrep[slab_a[0] * A + row_id // O] ^ occ_irrep[row_id % O]
        partner = occ ^ label
        low = jnp.zeros((1, O), jnp.int32)
        high = jnp.zeros((1, O), jnp.int32)
        for g in range(8):
            low = jnp.where(partner == g, starts[g : g + 1, :O], low)
            high = jnp.where(partner == g, starts[g + 1 : g + 2, :O], high)
        c_index = lax.broadcasted_iota(jnp.int32, (V, O), 0)
        kept = (c_index >= low) & (c_index < high)
        row[j, :, :O] = jnp.where(kept, amplitudes[j].astype(F32), 0.0)
    for j in range(STEP):
        left = jnp.concatenate(
            [row[j, pl.ds(u, V // GROUP, stride=GROUP), :].astype(BF) for u in range(GROUP)], axis=1
        )
        total = jnp.dot(left, chosen[...], preferred_element_type=F32)
        packed[pl.ds(step * STEP + j, V // GROUP, stride=16), :] = total

    @pl.when(step == ROWS // STEP - 1)
    def _():
        rows = PARTS * 16
        for e in range(NEAR):
            for far in range(FAR):
                first = (far * NEAR + e) * rows
                out[e, far * rows : (far + 1) * rows] = packed[first : first + rows].astype(BF)


def slot_owner(place, slot):
    _, rep = place()
    return ((rep // 2 + (REP // 2 - slot // 2)) % (REP // 2)) * 2 + (rep + slot) % 2


def multiply(place, vir_irrep, slab_a, slab_b, occ_row, amps, *rest):
    ints, (out, left, held, sems) = rest[:REP], rest[REP:]
    red, rep = place()
    copies = [pltpu.make_async_copy(ints[slot], held.at[slot], sems.at[slot]) for slot in range(REP)]
    for copy in copies:
        copy.start()
    occ = occ_row[...]
    rows = NEAR * 16
    for s in range(NEAR):
        for block in range(FAR * PARTS):
            left[s * 16 : (s + 1) * 16, block * LANES : (block + 1) * LANES] = amps[
                s, block * 16 : (block + 1) * 16
            ]
    _, _, pos_col = positions(occ)
    occ_lanes = jnp.concatenate([occ, jnp.full((1, LANES - O), 64, jnp.int32)], axis=1)
    pos_lanes = jnp.concatenate([pos_col, jnp.full((LANES - O, 1), -4 * LANES, jnp.int32)], axis=0)
    row = lax.broadcasted_iota(jnp.int32, (rows, LANES), 0)
    local = (row // 16) * ROWS + row % 16
    second = local >= O
    i_index = jnp.where(second, local - O, local)
    i_label = jnp.zeros((rows, LANES), jnp.int32)
    for g in range(1, 8):
        start = jnp.sum(jnp.where(occ < g, 1.0, 0.0), axis=1, keepdims=True).astype(jnp.int32)
        i_label += jnp.where(i_index >= start, 1, 0)
    a_first = slab_a[0] * A + (rep * FAR + red // NEAR) * 2
    row_label = i_label ^ jnp.where(second, vir_irrep[a_first + 1], vir_irrep[a_first])
    wanted = row_label ^ occ_lanes
    lane = lax.broadcasted_iota(jnp.int32, (LANES, 2 * LANES), 1)
    total = jnp.zeros((rows, 2 * LANES), F32)
    for pair in range(REP // 2):
        copies[2 * pair].wait()
        copies[2 * pair + 1].wait()
        right = jnp.concatenate([held[2 * pair], held[2 * pair + 1]], axis=1)
        both = jnp.dot(left[...], right, preferred_element_type=F32)
        for half in range(2):
            slot = 2 * pair + half
            b_label = vir_irrep[slab_b[0] * B + slot_owner(place, slot)]
            part = both[:, half * LANES : (half + 1) * LANES]
            part = jnp.where(wanted == b_label, part, 0.0)
            pick = jnp.where(lane == pos_lanes + SLOTS * slot, 1.0, 0.0).astype(BF)
            for piece in thirds(part):
                total += jnp.dot(piece, pick, preferred_element_type=F32)
    rest = total[:, LANES:]
    moved = pltpu.roll(rest, LANES // 2, 1)
    for e in range(NEAR):
        out[e, :16] = total[e * 16 : (e + 1) * 16, :LANES]
        out[e, 16:] = rest[e * 16 : e * 16 + 8] + moved[e * 16 + 8 : e * 16 + 16]


def finish(
    place, vir_irrep, occ_irrep, slab_a, slab_b, occ_energy, vir_energy, occ_row, energy_row, parts, other, out, cycle
):
    red, rep = place()
    occ = occ_row[...]
    _, pos_row, _ = positions(occ)
    total = parts[0]
    for s in range(1, NEAR):
        total += parts[s]
    main = total[:16]
    rest = jnp.concatenate([total[16:], pltpu.roll(total[16:], LANES // 2, 1)], axis=0)
    mains = jnp.concatenate(thirds(main), axis=0)
    rests = jnp.concatenate(thirds(rest), axis=0)
    lane = lax.broadcasted_iota(jnp.int32, (LANES, O), 0)
    for slot in range(REP):
        value = jnp.zeros((48, O), F32)
        if SLOTS * slot < LANES:
            pick = jnp.where(lane == pos_row + SLOTS * slot, 1.0, 0.0).astype(BF)
            value += jnp.dot(mains, pick, preferred_element_type=F32)
        if SLOTS * (slot + 1) > LANES:
            at = pos_row + (SLOTS * slot - LANES)
            pick = jnp.where((lane == at) & (lane < LANES // 2), 1.0, 0.0).astype(BF)
            value += jnp.dot(rests, pick, preferred_element_type=F32)
        cycle[pl.ds(slot_owner(place, slot), 16, stride=B), :O] = (value[:16] + value[16:32]) + value[32:]
    b_first = slab_b[0] * B
    b_index = lax.broadcasted_iota(jnp.int32, (B, 1), 0)
    b_label = jnp.zeros((B, 1), jnp.int32)
    b_energy = jnp.zeros((B, 1), F32)
    for b in range(B):
        b_label = jnp.where(b_index == b, vir_irrep[b_first + b], b_label)
        b_energy = jnp.where(b_index == b, vir_energy[b_first + b], b_energy)
    pair_bj = b_label ^ occ
    col_energy = energy_row[...] - b_energy
    for r in range(ROWS):
        row_id = (rep * (FAR * NEAR) + red) * ROWS + r
        a = slab_a[0] * A + row_id // O
        i = row_id % O
        label = vir_irrep[a] ^ occ_irrep[i]
        row_energy = occ_energy[i] - vir_energy[a]
        updated = (cycle[r * B : (r + 1) * B, :O] + other[r]) / (row_energy + col_energy)
        out[r] = jnp.where(pair_bj == label, updated, 0.0)


def own_place():
    return (
        lax.axis_index("far") * NEAR + lax.axis_index("near"),
        lax.axis_index("x") * 2 + lax.axis_index("core"),
    )


SMEM = pl.BlockSpec(memory_space=pltpu.SMEM)
VMEM = pl.BlockSpec(memory_space=pltpu.VMEM)


def params(limit):
    return pltpu.CompilerParams(vmem_limit_bytes=limit * 1024 * 1024)


def call_pack_integrals(place, vir_irrep, slab_b, occ_row, integrals, **kw):
    return pl.pallas_call(
        functools.partial(pack_integrals, place),
        out_shape=jax.ShapeDtypeStruct((FAR, PARTS * LANES, LANES), BF),
        in_specs=[SMEM, SMEM, VMEM, VMEM],
        out_specs=VMEM,
        scratch_shapes=[pltpu.VMEM((PARTS * LANES, LANES), F32)],
        compiler_params=params(16),
        cost_estimate=pl.CostEstimate(flops=2 * 10**7, bytes_accessed=600000, transcendentals=0),
        name="pack_integrals",
        **kw,
    )(vir_irrep, slab_b, occ_row, integrals)


def fixed(shape):
    return pl.BlockSpec(shape, lambda step: (0,) * len(shape))


def call_pack_amplitudes(place, vir_irrep, occ_irrep, slab_a, occ_row, vir_rows, amplitudes, **kw):
    return pl.pallas_call(
        functools.partial(pack_amplitudes, place),
        out_shape=(
            jax.ShapeDtypeStruct((NEAR, FAR * PARTS * 16, LANES), BF),
            jax.ShapeDtypeStruct((1, 1), jnp.int32),
        ),
        grid=(ROWS // STEP,),
        in_specs=[SMEM, SMEM, SMEM, fixed((1, O)), fixed((B, O)), pl.BlockSpec((STEP, V, O), lambda r: (r, 0, 0))],
        out_specs=(fixed((NEAR, FAR * PARTS * 16, LANES)), SMEM),
        scratch_shapes=[
            pltpu.VMEM((16, LANES), jnp.int32),
            pltpu.VMEM((GROUP * LANES, LANES), BF),
            pltpu.VMEM((STEP, V, LANES), F32),
            pltpu.VMEM((V // GROUP * 16, LANES), F32),
        ],
        compiler_params=params(32),
        cost_estimate=pl.CostEstimate(flops=10**9, bytes_accessed=4500000, transcendentals=0),
        name="pack_amplitudes",
        **kw,
    )(vir_irrep, occ_irrep, slab_a, occ_row, vir_rows, amplitudes)


def call_multiply(place, vir_irrep, slab_a, slab_b, occ_row, amps, ints, **kw):
    depth = FAR * PARTS * LANES
    return pl.pallas_call(
        functools.partial(multiply, place),
        out_shape=jax.ShapeDtypeStruct((NEAR, 24, LANES), F32),
        in_specs=[SMEM, SMEM, SMEM, VMEM, VMEM] + [pl.BlockSpec(memory_space=pl.ANY)] * REP,
        out_specs=VMEM,
        scratch_shapes=[
            pltpu.VMEM((NEAR * 16, depth), BF),
            pltpu.VMEM((REP, depth, LANES), BF),
            pltpu.SemaphoreType.DMA((REP,)),
        ],
        compiler_params=params(32),
        name="multiply",
        **kw,
    )(vir_irrep, slab_a, slab_b, occ_row, amps, *ints)


def call_finish(place, vir_irrep, occ_irrep, slab_a, slab_b, occ_energy, vir_energy, occ_row, energy_row, parts, other, **kw):
    return pl.pallas_call(
        functools.partial(finish, place),
        out_shape=jax.ShapeDtypeStruct((ROWS, B, O), F32),
        in_specs=[SMEM] * 6 + [VMEM] * 4,
        out_specs=VMEM,
        scratch_shapes=[pltpu.VMEM((16 * B, LANES), F32)],
        compiler_params=params(16),
        name="finish",
        **kw,
    )(vir_irrep, occ_irrep, slab_a, slab_b, occ_energy, vir_energy, occ_row, energy_row, parts, other)


def whole_form(amplitudes, integrals, other_terms, occ_energy, vir_energy, occ_irrep, vir_irrep, slab_a, slab_b):
    red, rep = ("far", "near"), ("x", "core")
    red_count = FAR * NEAR
    red_index, rep_index = own_place()
    a_start = slab_a[0] * A
    b_start = slab_b[0] * B
    b_labels = lax.dynamic_slice_in_dim(vir_irrep, b_start, B)
    b_energy = lax.dynamic_slice_in_dim(vir_energy, b_start, B)
    c_labels = lax.dynamic_slice_in_dim(vir_irrep, red_index * ROWS, ROWS)
    pair_ck = pair_labels(c_labels, occ_irrep)
    pair_bj = pair_labels(b_labels, occ_irrep)
    own_pairs = lax.dynamic_slice_in_dim(pair_bj, rep_index, 1, 0)
    local_kept = (pair_ck[:, :, None, None] == own_pairs[None, None]).astype(BF)
    kept = (integrals * local_kept).reshape(1, ROWS * O, O)
    gathered = lax.all_to_all(jnp.broadcast_to(kept, (REP, ROWS * O, O)), rep, 0, 0, tiled=True)
    exchanged = lax.all_to_all(amplitudes, red, split_axis=1, concat_axis=0, tiled=True)
    flat_amps = exchanged.reshape(red_count * ROWS, ROWS * O)
    flat_ints = jnp.swapaxes(gathered, 0, 1).reshape(ROWS * O, B * O)
    parts = jnp.dot(flat_amps, flat_ints, preferred_element_type=F32).reshape(red_count, ROWS, B * O)
    mine = jnp.sum(lax.all_to_all(parts, red, 0, 0, tiled=True), axis=0)
    cycle_term = mine.reshape(ROWS, B, O)
    first_global = (rep_index * red_count + red_index) * ROWS
    row_ids = first_global + jnp.arange(ROWS, dtype=jnp.int32)
    a_index = a_start + row_ids // O
    i_index = row_ids % O
    pair_ai = jnp.bitwise_xor(vir_irrep[a_index], occ_irrep[i_index])
    allowed = pair_ai[:, None, None] == pair_bj[None]
    row_energy = occ_energy[i_index] - vir_energy[a_index]
    col_energy = occ_energy[None, :] - b_energy[:, None]
    denominator = row_energy[:, None, None] + col_energy[None]
    updated = (cycle_term + other_terms) / denominator
    return jnp.where(allowed, updated, jnp.zeros_like(updated))


def on_device(
    amplitudes, integrals, other_terms, occ_energy, vir_energy, occ_irrep, vir_irrep, slab_a, slab_b
):
    occ_row = occ_irrep.reshape(1, O)
    vir_rows = vir_irrep.reshape(B, O)
    ints = call_pack_integrals(own_place, vir_irrep, slab_b, occ_row, integrals.reshape(ROWS, O, O))
    ints = lax.all_to_all(ints, "far", 0, 0, tiled=True).reshape(FAR * PARTS * LANES, LANES)
    count = REP // 2
    held = [ints] + [lax.ppermute(ints, "x", [(i, (i + s) % count) for i in range(count)]) for s in range(1, count)]
    ints = [half for own in held for half in (own, lax.ppermute(own, "core", [(0, 1), (1, 0)]))]
    amps, most = call_pack_amplitudes(own_place, vir_irrep, occ_irrep, slab_a, occ_row, vir_rows, amplitudes)
    amps = lax.all_to_all(amps, "near", 0, 0, tiled=True)
    parts = call_multiply(own_place, vir_irrep, slab_a, slab_b, occ_row, amps, ints)
    parts = lax.all_to_all(parts, "near", 0, 0, tiled=True)

    def packed_form(amplitudes, integrals, *rest):
        other_terms, occ_energy, vir_energy, occ_irrep, vir_irrep, slab_a, slab_b, parts = rest
        return call_finish(
            own_place, vir_irrep, occ_irrep, slab_a, slab_b, occ_energy, vir_energy,
            occ_irrep.reshape(1, O), occ_energy.reshape(1, O), parts, other_terms,
        )

    return lax.cond(
        most[0, 0] >= SLOTS, lambda *args: whole_form(*args[:-1]), packed_form,
        amplitudes, integrals, other_terms, occ_energy, vir_energy, occ_irrep, vir_irrep, slab_a, slab_b, parts,
    )


def solution(mesh):
    split = Mesh(mesh.devices.reshape(FAR, NEAR, REP // 2, 2), ("far", "near", "x", "core"))
    rows = P(("x", "core", "far", "near"), None, None)
    placed = (
        rows,
        P(("far", "near"), None, ("x", "core"), None),
        rows,
        P(),
        P(),
        P(),
        P(),
        P(),
        P(),
    )
    return jax.shard_map(
        on_device,
        mesh=split,
        in_specs=placed,
        out_specs=rows,
        check_vma=False,
    )
```

```python
import functools

import jax
import jax.numpy as jnp
from jax import lax
from jax.experimental import pallas as pl
from jax.experimental.pallas import tpu as pltpu
from jax.sharding import Mesh, PartitionSpec as P

A = 64
B = 8
O = 120
V = 960
ROWS = 15
SLOTS = 24
GROUP = 5
PARTS = ROWS // GROUP
STEP = 5
FAR = 8
NEAR = 8
ACROSS = 4
SHARE = SLOTS // ACROSS
TEAM = NEAR * ACROSS
BLOCK = 32
STACK = 4
TWICE = FAR // STACK
DEEP = TWICE * PARTS
REP = 8
LANES = 128
BF = jnp.bfloat16
F32 = jnp.float32


def pair_labels(left, right):
    return jnp.bitwise_xor(left[:, None], right[None, :])


def column_of(row):
    n = row.shape[1]
    same = lax.broadcasted_iota(jnp.int32, (n, n), 0) == lax.broadcasted_iota(jnp.int32, (n, n), 1)
    return jnp.sum(jnp.where(same, row.astype(F32), 0.0), axis=1, keepdims=True).astype(jnp.int32)


def positions(occ_row):
    n = occ_row.shape[1]
    occ_col = column_of(occ_row)
    k_col = lax.broadcasted_iota(jnp.int32, (n, n), 0)
    k_row = lax.broadcasted_iota(jnp.int32, (n, n), 1)
    same = occ_col == occ_row
    row = jnp.sum(jnp.where(same & (k_col < k_row), 1.0, 0.0), axis=0, keepdims=True)
    col = jnp.sum(jnp.where(same & (k_row < k_col), 1.0, 0.0), axis=1, keepdims=True)
    return occ_col, row.astype(jnp.int32), col.astype(jnp.int32)


def thirds(x):
    high = x.astype(BF)
    rest = x - high.astype(F32)
    middle = rest.astype(BF)
    low = (rest - middle.astype(F32)).astype(BF)
    return high, middle, low


def pack_integrals(place, vir_irrep, slab_b, occ_row, integrals, out, most, scratch):
    red, rep = place()
    occ = occ_row[...]
    occ_col, pos_row, _ = positions(occ)
    most[0, 0] = jnp.max(pos_row)
    slot = lax.broadcasted_iota(jnp.int32, (SLOTS, O), 0)
    pick = jnp.where(slot == pos_row, 1.0, 0.0).astype(BF)
    b_label = vir_irrep[slab_b[0] * B + rep]
    scratch[...] = jnp.zeros_like(scratch)
    for c in range(ROWS):
        label = vir_irrep[red * ROWS + c] ^ b_label
        kept = jnp.where((occ_col ^ label) == occ, integrals[c].astype(F32), 0.0).astype(BF)
        slots = jnp.dot(pick, kept, preferred_element_type=F32)
        for x in range(ACROSS):
            first = (x * PARTS + c // GROUP) * BLOCK + SHARE * (c % GROUP)
            scratch[first : first + SHARE, :O] = slots[x * SHARE : (x + 1) * SHARE]
    for x in range(ACROSS):
        out[x] = scratch[x * PARTS * BLOCK : (x + 1) * PARTS * BLOCK].astype(BF)


def pack_amplitudes(
    place, vir_irrep, occ_irrep, slab_a, occ_row, vir_rows, amplitudes, out, starts, chosen, row, packed
):
    red, rep = place()
    step = pl.program_id(0)
    occ = occ_row[...]
    groups = V // GROUP // STACK
    part = NEAR * PARTS

    @pl.when(step == 0)
    def _():
        _, _, pos_col = positions(occ)
        lane = lax.broadcasted_iota(jnp.int32, (O, LANES), 1)
        chosen[...] = jnp.zeros_like(chosen)
        at = pos_col
        for x in range(1, ACROSS):
            at += jnp.where(pos_col >= x * SHARE, BLOCK - SHARE, 0)
        for u in range(GROUP):
            hit = (lane == at + SHARE * u) & (pos_col < SLOTS)
            chosen[u * LANES : u * LANES + O] = jnp.where(hit, 1.0, 0.0).astype(BF)
        labels = vir_rows[...]
        for g in range(9):
            below = jnp.sum(jnp.where(labels < g, 1.0, 0.0), axis=1, keepdims=True)
            starts[g : g + 1] = jnp.broadcast_to(below.astype(jnp.int32), (1, LANES))
        for x in range(ACROSS):
            packed[x, pl.ds(ROWS, groups, stride=16), :] = jnp.zeros((groups, LANES), F32)
        row[...] = jnp.zeros_like(row)

    for j in range(STEP):
        row_id = (rep * (FAR * NEAR) + red) * ROWS + step * STEP + j
        label = vir_irrep[slab_a[0] * A + row_id // O] ^ occ_irrep[row_id % O]
        partner = occ ^ label
        low = jnp.zeros((1, O), jnp.int32)
        high = jnp.zeros((1, O), jnp.int32)
        for g in range(8):
            low = jnp.where(partner == g, starts[g : g + 1, :O], low)
            high = jnp.where(partner == g, starts[g + 1 : g + 2, :O], high)
        c_index = lax.broadcasted_iota(jnp.int32, (V, O), 0)
        kept = (c_index >= low) & (c_index < high)
        row[j, :, :O] = jnp.where(kept, amplitudes[j].astype(F32), 0.0)
    for j in range(STEP):
        left = jnp.concatenate(
            [row[j, pl.ds(u, V // GROUP, stride=GROUP), :].astype(BF) for u in range(GROUP)], axis=1
        )
        total = jnp.dot(left, chosen[...], preferred_element_type=F32)
        blocks = [
            jnp.concatenate([total[(STACK * t + f) * part : (STACK * t + f + 1) * part] for t in range(TWICE)], axis=0)
            for f in range(STACK)
        ]
        place_of = lax.broadcasted_iota(jnp.int32, (groups, LANES), 1) // BLOCK
        for x in range(ACROSS):
            tile = blocks[0] if x == 0 else pltpu.roll(blocks[0], (LANES - BLOCK * x), 1)
            for f in range(1, STACK):
                moved = blocks[f] if x == f else pltpu.roll(blocks[f], (LANES + BLOCK * (f - x)) % LANES, 1)
                tile = jnp.where(place_of == f, moved, tile)
            packed[x, pl.ds(step * STEP + j, groups, stride=16), :] = tile

    @pl.when(step == ROWS // STEP - 1)
    def _():
        rows = PARTS * 16
        for e in range(NEAR):
            for x in range(ACROSS):
                for t in range(TWICE):
                    first = (t * NEAR + e) * rows
                    out[ACROSS * e + x, t * rows : (t + 1) * rows] = packed[x, first : first + rows].astype(BF)


def slot_owner(place, slot):
    _, rep = place()
    return slot % ACROSS * 2 + (rep + slot // ACROSS) % 2


def multiply(place, vir_irrep, slab_a, slab_b, occ_row, amps, *rest):
    ints, (out, kept, picks) = rest[:2], rest[2:]
    red, rep = place()
    occ = occ_row[...]
    rows = TEAM * 16
    left = jnp.concatenate([amps[:, k * 16 : (k + 1) * 16].reshape(rows, LANES) for k in range(DEEP)], axis=1)
    _, _, pos_col = positions(occ)
    occ_lanes = jnp.concatenate([occ, jnp.full((1, LANES - O), 64, jnp.int32)], axis=1)
    pos_lanes = jnp.concatenate([pos_col, jnp.full((LANES - O, 1), -4 * LANES, jnp.int32)], axis=0)
    row = lax.broadcasted_iota(jnp.int32, (rows, LANES), 0)
    i_index = (row // (16 * ACROSS)) * ROWS + row % 16
    row_label = jnp.zeros((rows, LANES), jnp.int32)
    for g in range(1, 8):
        start = jnp.sum(jnp.where(occ < g, 1.0, 0.0), axis=1, keepdims=True).astype(jnp.int32)
        row_label += jnp.where(i_index >= start, 1, 0)
    a_label = jnp.zeros((rows, LANES), jnp.int32)
    for x in range(ACROSS):
        label = vir_irrep[slab_a[0] * A + (x * 2 + rep % 2) * FAR + red // NEAR]
        a_label = jnp.where((row // 16) % ACROSS == x, label, a_label)
    row_label = row_label ^ a_label
    wanted = row_label ^ occ_lanes
    lane = lax.broadcasted_iota(jnp.int32, (LANES, 2 * LANES), 1)
    for slot in range(REP):
        pick = jnp.where(lane == pos_lanes + SLOTS * slot, 1.0, 0.0).astype(BF)
        for piece in range(2):
            first = (2 * slot + piece) * LANES
            picks[first : first + LANES] = pick
    for pair in range(REP // 2):
        held = ints[pair * 2 // ACROSS]
        across = (pair * 2 % ACROSS, pair * 2 % ACROSS + 1)
        right = jnp.concatenate(
            [
                jnp.concatenate([held[far, x, g * BLOCK : (g + 1) * BLOCK] for x in across], axis=1)
                for t in range(TWICE)
                for g in range(PARTS)
                for far in range(t * STACK, (t + 1) * STACK)
            ],
            axis=0,
        )
        both = jnp.dot(left, right, preferred_element_type=F32)
        for half in range(2):
            slot = 2 * pair + half
            b_label = vir_irrep[slab_b[0] * B + slot_owner(place, slot)]
            part = both[:, half * LANES : (half + 1) * LANES]
            part = jnp.where(wanted == b_label, part, 0.0)
            high = part.astype(BF)
            first = 2 * slot * LANES
            kept[:, first : first + LANES] = high
            kept[:, first + LANES : first + 2 * LANES] = (part - high.astype(F32)).astype(BF)
    total = jnp.dot(kept[...], picks[...], preferred_element_type=F32)
    rest = total[:, LANES:]
    moved = pltpu.roll(rest, LANES // 2, 1)
    for e in range(TEAM):
        out[e, :16] = total[e * 16 : (e + 1) * 16, :LANES]
        out[e, 16:] = rest[e * 16 : e * 16 + 8] + moved[e * 16 + 8 : e * 16 + 16]


def finish(
    place, vir_irrep, occ_irrep, slab_a, slab_b, occ_energy, vir_energy, occ_row, energy_row, parts, other, out, cycle
):
    red, rep = place()
    occ = occ_row[...]
    _, pos_row, _ = positions(occ)
    total = parts[0]
    for s in range(1, TEAM):
        total += parts[s]
    main = total[:16]
    rest = jnp.concatenate([total[16:], pltpu.roll(total[16:], LANES // 2, 1)], axis=0)
    mains = jnp.concatenate(thirds(main), axis=0)
    rests = jnp.concatenate(thirds(rest), axis=0)
    lane = lax.broadcasted_iota(jnp.int32, (LANES, O), 0)
    for slot in range(REP):
        value = jnp.zeros((48, O), F32)
        if SLOTS * slot < LANES:
            pick = jnp.where(lane == pos_row + SLOTS * slot, 1.0, 0.0).astype(BF)
            value += jnp.dot(mains, pick, preferred_element_type=F32)
        if SLOTS * (slot + 1) > LANES:
            at = pos_row + (SLOTS * slot - LANES)
            pick = jnp.where((lane == at) & (lane < LANES // 2), 1.0, 0.0).astype(BF)
            value += jnp.dot(rests, pick, preferred_element_type=F32)
        cycle[pl.ds(slot_owner(place, slot), 16, stride=B), :O] = (value[:16] + value[16:32]) + value[32:]
    b_first = slab_b[0] * B
    b_index = lax.broadcasted_iota(jnp.int32, (B, 1), 0)
    b_label = jnp.zeros((B, 1), jnp.int32)
    b_energy = jnp.zeros((B, 1), F32)
    for b in range(B):
        b_label = jnp.where(b_index == b, vir_irrep[b_first + b], b_label)
        b_energy = jnp.where(b_index == b, vir_energy[b_first + b], b_energy)
    pair_bj = b_label ^ occ
    col_energy = energy_row[...] - b_energy
    for r in range(ROWS):
        row_id = (rep * (FAR * NEAR) + red) * ROWS + r
        a = slab_a[0] * A + row_id // O
        i = row_id % O
        label = vir_irrep[a] ^ occ_irrep[i]
        row_energy = occ_energy[i] - vir_energy[a]
        updated = (cycle[r * B : (r + 1) * B, :O] + other[r]) / (row_energy + col_energy)
        out[r] = jnp.where(pair_bj == label, updated, 0.0)


def own_place():
    return (
        lax.axis_index("far") * NEAR + lax.axis_index("near"),
        lax.axis_index("x") * 2 + lax.axis_index("core"),
    )


SMEM = pl.BlockSpec(memory_space=pltpu.SMEM)
VMEM = pl.BlockSpec(memory_space=pltpu.VMEM)


def params(limit):
    return pltpu.CompilerParams(vmem_limit_bytes=limit * 1024 * 1024)


def call_pack_integrals(place, vir_irrep, slab_b, occ_row, integrals, **kw):
    return pl.pallas_call(
        functools.partial(pack_integrals, place),
        out_shape=(jax.ShapeDtypeStruct((ACROSS, PARTS * BLOCK, LANES), BF), jax.ShapeDtypeStruct((1, 1), jnp.int32)),
        in_specs=[SMEM, SMEM, VMEM, VMEM],
        out_specs=(VMEM, SMEM),
        scratch_shapes=[pltpu.VMEM((ACROSS * PARTS * BLOCK, LANES), F32)],
        compiler_params=params(16),
        cost_estimate=pl.CostEstimate(flops=2 * 10**7, bytes_accessed=600000, transcendentals=0),
        name="pack_integrals",
        **kw,
    )(vir_irrep, slab_b, occ_row, integrals)


def fixed(shape):
    return pl.BlockSpec(shape, lambda step: (0,) * len(shape))


def call_pack_amplitudes(place, vir_irrep, occ_irrep, slab_a, occ_row, vir_rows, amplitudes, **kw):
    return pl.pallas_call(
        functools.partial(pack_amplitudes, place),
        out_shape=jax.ShapeDtypeStruct((TEAM, DEEP * 16, LANES), BF),
        grid=(ROWS // STEP,),
        in_specs=[SMEM, SMEM, SMEM, fixed((1, O)), fixed((1, V)), pl.BlockSpec((STEP, V, O), lambda r: (r, 0, 0))],
        out_specs=fixed((TEAM, DEEP * 16, LANES)),
        scratch_shapes=[
            pltpu.VMEM((16, LANES), jnp.int32),
            pltpu.VMEM((GROUP * LANES, LANES), BF),
            pltpu.VMEM((STEP, V, LANES), F32),
            pltpu.VMEM((ACROSS, V // GROUP // STACK * 16, LANES), F32),
        ],
        compiler_params=params(16),
        cost_estimate=pl.CostEstimate(flops=10**9, bytes_accessed=4500000, transcendentals=0),
        name="pack_amplitudes",
        **kw,
    )(vir_irrep, occ_irrep, slab_a, occ_row, vir_rows, amplitudes)


def call_multiply(place, vir_irrep, slab_a, slab_b, occ_row, amps, ints, **kw):
    return pl.pallas_call(
        functools.partial(multiply, place),
        out_shape=jax.ShapeDtypeStruct((TEAM, 24, LANES), F32),
        in_specs=[SMEM, SMEM, SMEM, VMEM, VMEM] + [VMEM] * 2,
        out_specs=VMEM,
        scratch_shapes=[
            pltpu.VMEM((TEAM * 16, 2 * REP * LANES), BF),
            pltpu.VMEM((2 * REP * LANES, 2 * LANES), BF),
        ],
        compiler_params=params(24),
        name="multiply",
        **kw,
    )(vir_irrep, slab_a, slab_b, occ_row, amps, *ints)


def call_finish(place, vir_irrep, occ_irrep, slab_a, slab_b, occ_energy, vir_energy, occ_row, energy_row, parts, other, **kw):
    return pl.pallas_call(
        functools.partial(finish, place),
        out_shape=jax.ShapeDtypeStruct((ROWS, B, O), F32),
        in_specs=[SMEM] * 6 + [VMEM] * 4,
        out_specs=VMEM,
        scratch_shapes=[pltpu.VMEM((16 * B, LANES), F32)],
        compiler_params=params(16),
        name="finish",
        **kw,
    )(vir_irrep, occ_irrep, slab_a, slab_b, occ_energy, vir_energy, occ_row, energy_row, parts, other)


def whole_form(amplitudes, integrals, other_terms, occ_energy, vir_energy, occ_irrep, vir_irrep, slab_a, slab_b):
    red, rep = ("far", "near"), ("x", "core")
    red_count = FAR * NEAR
    red_index, rep_index = own_place()
    a_start = slab_a[0] * A
    b_start = slab_b[0] * B
    b_labels = lax.dynamic_slice_in_dim(vir_irrep, b_start, B)
    b_energy = lax.dynamic_slice_in_dim(vir_energy, b_start, B)
    c_labels = lax.dynamic_slice_in_dim(vir_irrep, red_index * ROWS, ROWS)
    pair_ck = pair_labels(c_labels, occ_irrep)
    pair_bj = pair_labels(b_labels, occ_irrep)
    own_pairs = lax.dynamic_slice_in_dim(pair_bj, rep_index, 1, 0)
    local_kept = (pair_ck[:, :, None, None] == own_pairs[None, None]).astype(BF)
    kept = (integrals * local_kept).reshape(1, ROWS * O, O)
    gathered = lax.all_to_all(jnp.broadcast_to(kept, (REP, ROWS * O, O)), rep, 0, 0, tiled=True)
    exchanged = lax.all_to_all(amplitudes, red, split_axis=1, concat_axis=0, tiled=True)
    flat_amps = exchanged.reshape(red_count * ROWS, ROWS * O)
    flat_ints = jnp.swapaxes(gathered, 0, 1).reshape(ROWS * O, B * O)
    parts = jnp.dot(flat_amps, flat_ints, preferred_element_type=F32).reshape(red_count, ROWS, B * O)
    mine = jnp.sum(lax.all_to_all(parts, red, 0, 0, tiled=True), axis=0)
    cycle_term = mine.reshape(ROWS, B, O)
    first_global = (rep_index * red_count + red_index) * ROWS
    row_ids = first_global + jnp.arange(ROWS, dtype=jnp.int32)
    a_index = a_start + row_ids // O
    i_index = row_ids % O
    pair_ai = jnp.bitwise_xor(vir_irrep[a_index], occ_irrep[i_index])
    allowed = pair_ai[:, None, None] == pair_bj[None]
    row_energy = occ_energy[i_index] - vir_energy[a_index]
    col_energy = occ_energy[None, :] - b_energy[:, None]
    denominator = row_energy[:, None, None] + col_energy[None]
    updated = (cycle_term + other_terms) / denominator
    return jnp.where(allowed, updated, jnp.zeros_like(updated))


def packed_form(
    amplitudes, integrals, other_terms, occ_energy, vir_energy, occ_irrep, vir_irrep, slab_a, slab_b, ints
):
    occ_row = occ_irrep.reshape(1, O)
    vir_rows = vir_irrep.reshape(1, V)
    ints = lax.all_to_all(ints, "x", 0, 0, tiled=True)
    amps = call_pack_amplitudes(own_place, vir_irrep, occ_irrep, slab_a, occ_row, vir_rows, amplitudes)
    ints = lax.all_gather(ints, "far", axis=0)
    ints, amps = lax.optimization_barrier((ints, amps))
    ints = [ints, lax.ppermute(ints, "core", [(0, 1), (1, 0)])]
    amps = lax.all_to_all(amps, ("near", "x"), 0, 0, tiled=True)
    parts = call_multiply(own_place, vir_irrep, slab_a, slab_b, occ_row, amps, ints)
    parts = lax.all_to_all(parts, ("near", "x"), 0, 0, tiled=True)
    return call_finish(
        own_place, vir_irrep, occ_irrep, slab_a, slab_b, occ_energy, vir_energy,
        occ_row, occ_energy.reshape(1, O), parts, other_terms,
    )


def on_device(
    amplitudes, integrals, other_terms, occ_energy, vir_energy, occ_irrep, vir_irrep, slab_a, slab_b
):
    args = (amplitudes, integrals, other_terms, occ_energy, vir_energy, occ_irrep, vir_irrep, slab_a, slab_b)
    ints, most = call_pack_integrals(
        own_place, vir_irrep, slab_b, occ_irrep.reshape(1, O), integrals.reshape(ROWS, O, O)
    )
    return lax.cond(most[0, 0] >= SLOTS, lambda *rest: whole_form(*rest[:-1]), packed_form, *args, ints)


def solution(mesh):
    split = Mesh(mesh.devices.reshape(FAR, NEAR, ACROSS, 2), ("far", "near", "x", "core"))
    rows = P(("x", "core", "far", "near"), None, None)
    placed = (
        rows,
        P(("far", "near"), None, ("x", "core"), None),
        rows,
        P(),
        P(),
        P(),
        P(),
        P(),
        P(),
    )
    return jax.shard_map(
        on_device,
        mesh=split,
        in_specs=placed,
        out_specs=rows,
        check_vma=False,
    )
```

```python
import functools

import jax
import jax.numpy as jnp
from jax import lax
from jax.experimental import pallas as pl
from jax.experimental.pallas import tpu as pltpu
from jax.sharding import Mesh, PartitionSpec as P

A = 64
B = 8
O = 120
V = 960
ROWS = 15
SLOTS = 24
GROUP = 5
PARTS = ROWS // GROUP
STEP = 5
FAR = 8
NEAR = 8
ACROSS = 4
SHARE = SLOTS // ACROSS
TEAM = NEAR * ACROSS
BLOCK = 32
STACK = 4
TWICE = FAR // STACK
DEEP = TWICE * PARTS
REP = 8
LANES = 128
BF = jnp.bfloat16
F32 = jnp.float32


def pair_labels(left, right):
    return jnp.bitwise_xor(left[:, None], right[None, :])


def column_of(row):
    n = row.shape[1]
    same = lax.broadcasted_iota(jnp.int32, (n, n), 0) == lax.broadcasted_iota(jnp.int32, (n, n), 1)
    return jnp.sum(jnp.where(same, row.astype(F32), 0.0), axis=1, keepdims=True).astype(jnp.int32)


def positions(occ_row):
    n = occ_row.shape[1]
    occ_col = column_of(occ_row)
    k_col = lax.broadcasted_iota(jnp.int32, (n, n), 0)
    k_row = lax.broadcasted_iota(jnp.int32, (n, n), 1)
    same = occ_col == occ_row
    row = jnp.sum(jnp.where(same & (k_col < k_row), 1.0, 0.0), axis=0, keepdims=True)
    col = jnp.sum(jnp.where(same & (k_row < k_col), 1.0, 0.0), axis=1, keepdims=True)
    return occ_col, row.astype(jnp.int32), col.astype(jnp.int32)


def thirds(x):
    high = x.astype(BF)
    rest = x - high.astype(F32)
    middle = rest.astype(BF)
    low = (rest - middle.astype(F32)).astype(BF)
    return high, middle, low


def pack_integrals(place, window, vir_irrep, slab_b, occ_row, integrals, out, most, scratch):
    red, rep = place()
    occ = occ_row[...]
    occ_col, pos_row, _ = positions(occ)
    most[0, 0] = jnp.max(pos_row)
    slot = lax.broadcasted_iota(jnp.int32, (SLOTS, O), 0)
    pick = jnp.where(slot == pos_row - SLOTS * window, 1.0, 0.0).astype(BF)
    b_label = vir_irrep[slab_b[0] * B + rep]
    scratch[...] = jnp.zeros_like(scratch)
    for c in range(ROWS):
        label = vir_irrep[red * ROWS + c] ^ b_label
        kept = jnp.where((occ_col ^ label) == occ, integrals[c].astype(F32), 0.0).astype(BF)
        slots = jnp.dot(pick, kept, preferred_element_type=F32)
        for x in range(ACROSS):
            first = (x * PARTS + c // GROUP) * BLOCK + SHARE * (c % GROUP)
            scratch[first : first + SHARE, :O] = slots[x * SHARE : (x + 1) * SHARE]
    for x in range(ACROSS):
        out[x] = scratch[x * PARTS * BLOCK : (x + 1) * PARTS * BLOCK].astype(BF)


def pack_amplitudes(
    place, window, vir_irrep, occ_irrep, slab_a, occ_row, vir_rows, amplitudes, out, starts, chosen, row, packed
):
    red, rep = place()
    step = pl.program_id(0)
    occ = occ_row[...]
    groups = V // GROUP // STACK
    part = NEAR * PARTS

    @pl.when(step == 0)
    def _():
        _, _, pos_col = positions(occ)
        pos_col -= SLOTS * window
        lane = lax.broadcasted_iota(jnp.int32, (O, LANES), 1)
        chosen[...] = jnp.zeros_like(chosen)
        at = pos_col
        for x in range(1, ACROSS):
            at += jnp.where(pos_col >= x * SHARE, BLOCK - SHARE, 0)
        for u in range(GROUP):
            hit = (lane == at + SHARE * u) & (pos_col >= 0) & (pos_col < SLOTS)
            chosen[u * LANES : u * LANES + O] = jnp.where(hit, 1.0, 0.0).astype(BF)
        labels = vir_rows[...]
        for g in range(9):
            below = jnp.sum(jnp.where(labels < g, 1.0, 0.0), axis=1, keepdims=True)
            starts[g : g + 1] = jnp.broadcast_to(below.astype(jnp.int32), (1, LANES))
        for x in range(ACROSS):
            packed[x, pl.ds(ROWS, groups, stride=16), :] = jnp.zeros((groups, LANES), F32)
        row[...] = jnp.zeros_like(row)

    c_index = lax.broadcasted_iota(jnp.int16, (V, O), 0)
    for j in range(STEP):
        row_id = (rep * (FAR * NEAR) + red) * ROWS + step * STEP + j
        label = vir_irrep[slab_a[0] * A + row_id // O] ^ occ_irrep[row_id % O]
        partner = occ ^ label
        low = jnp.zeros((1, O), jnp.int32)
        high = jnp.zeros((1, O), jnp.int32)
        for g in range(8):
            low = jnp.where(partner == g, starts[g : g + 1, :O], low)
            high = jnp.where(partner == g, starts[g + 1 : g + 2, :O], high)
        kept = (c_index >= low.astype(jnp.int16)) & (c_index < high.astype(jnp.int16))
        row[j, :, :O] = jnp.where(kept, amplitudes[j], jnp.zeros((), BF)).astype(F32)
    for j in range(STEP):
        left = jnp.concatenate(
            [row[j, pl.ds(u, V // GROUP, stride=GROUP), :].astype(BF) for u in range(GROUP)], axis=1
        )
        total = jnp.dot(left, chosen[...], preferred_element_type=F32)
        blocks = [
            jnp.concatenate([total[(STACK * t + f) * part : (STACK * t + f + 1) * part] for t in range(TWICE)], axis=0)
            for f in range(STACK)
        ]
        place_of = lax.broadcasted_iota(jnp.int32, (1, LANES), 1) // BLOCK
        for x in range(ACROSS):
            tile = blocks[0] if x == 0 else pltpu.roll(blocks[0], (LANES - BLOCK * x), 1)
            for f in range(1, STACK):
                moved = blocks[f] if x == f else pltpu.roll(blocks[f], (LANES + BLOCK * (f - x)) % LANES, 1)
                tile = jnp.where(place_of == f, moved, tile)
            packed[x, pl.ds(step * STEP + j, groups, stride=16), :] = tile

    @pl.when(step == ROWS // STEP - 1)
    def _():
        rows = PARTS * 16
        for e in range(NEAR):
            for x in range(ACROSS):
                for t in range(TWICE):
                    first = (t * NEAR + e) * rows
                    out[ACROSS * e + x, t * rows : (t + 1) * rows] = packed[x, first : first + rows].astype(BF)


def slot_owner(place, slot):
    _, rep = place()
    return slot % ACROSS * 2 + (rep + slot // ACROSS) % 2


def multiply(place, window, vir_irrep, slab_a, slab_b, occ_row, amps, *rest):
    ints, (out, kept, picks) = rest[:2], rest[2:]
    red, rep = place()
    occ = occ_row[...]
    rows = TEAM * 16
    left = jnp.concatenate([amps[:, k * 16 : (k + 1) * 16].reshape(rows, LANES) for k in range(DEEP)], axis=1)
    _, _, pos_col = positions(occ)
    occ_lanes = jnp.concatenate([occ, jnp.full((1, LANES - O), 64, jnp.int32)], axis=1)
    pos_col -= SLOTS * window
    pos_col = jnp.where((pos_col >= 0) & (pos_col < SLOTS), pos_col, -4 * LANES)
    pos_lanes = jnp.concatenate([pos_col, jnp.full((LANES - O, 1), -4 * LANES, jnp.int32)], axis=0)
    row = lax.broadcasted_iota(jnp.int32, (rows, LANES), 0)
    i_index = (row // (16 * ACROSS)) * ROWS + row % 16
    row_label = jnp.zeros((rows, LANES), jnp.int32)
    for g in range(1, 8):
        start = jnp.sum(jnp.where(occ < g, 1.0, 0.0), axis=1, keepdims=True).astype(jnp.int32)
        row_label += jnp.where(i_index >= start, 1, 0)
    a_label = jnp.zeros((rows, LANES), jnp.int32)
    for x in range(ACROSS):
        label = vir_irrep[slab_a[0] * A + (x * 2 + rep % 2) * FAR + red // NEAR]
        a_label = jnp.where((row // 16) % ACROSS == x, label, a_label)
    row_label = row_label ^ a_label
    wanted = row_label ^ occ_lanes
    lane = lax.broadcasted_iota(jnp.int32, (LANES, 2 * LANES), 1)
    for slot in range(REP):
        pick = jnp.where(lane == pos_lanes + SLOTS * slot, 1.0, 0.0).astype(BF)
        for piece in range(2):
            first = (2 * slot + piece) * LANES
            picks[first : first + LANES] = pick
    for pair in range(REP // 2):
        held = ints[pair * 2 // ACROSS]
        across = (pair * 2 % ACROSS, pair * 2 % ACROSS + 1)
        right = jnp.concatenate(
            [
                jnp.concatenate([held[far, x, g * BLOCK : (g + 1) * BLOCK] for x in across], axis=1)
                for t in range(TWICE)
                for g in range(PARTS)
                for far in range(t * STACK, (t + 1) * STACK)
            ],
            axis=0,
        )
        both = jnp.dot(left, right, preferred_element_type=F32)
        for half in range(2):
            slot = 2 * pair + half
            b_label = vir_irrep[slab_b[0] * B + slot_owner(place, slot)]
            part = both[:, half * LANES : (half + 1) * LANES]
            part = jnp.where(wanted == b_label, part, 0.0)
            high = part.astype(BF)
            first = 2 * slot * LANES
            kept[:, first : first + LANES] = high
            kept[:, first + LANES : first + 2 * LANES] = (part - high.astype(F32)).astype(BF)
    total = jnp.dot(kept[...], picks[...], preferred_element_type=F32)
    rest = total[:, LANES:]
    moved = pltpu.roll(rest, LANES // 2, 1)
    for e in range(TEAM):
        out[e, :16] = total[e * 16 : (e + 1) * 16, :LANES]
        out[e, 16:] = rest[e * 16 : e * 16 + 8] + moved[e * 16 + 8 : e * 16 + 16]


def finish(
    place, vir_irrep, occ_irrep, slab_a, slab_b, occ_energy, vir_energy, occ_row, energy_row, other, *rest
):
    windows, (out, cycle) = rest[:-2], rest[-2:]
    red, rep = place()
    occ = occ_row[...]
    _, pos_row, _ = positions(occ)
    lane = lax.broadcasted_iota(jnp.int32, (LANES, O), 0)
    values = [jnp.zeros((48, O), F32) for _ in range(REP)]
    for window, parts in enumerate(windows):
        total = parts[0]
        for s in range(1, TEAM):
            total += parts[s]
        main = total[:16]
        rest = jnp.concatenate([total[16:], pltpu.roll(total[16:], LANES // 2, 1)], axis=0)
        mains = jnp.concatenate(thirds(main), axis=0)
        rests = jnp.concatenate(thirds(rest), axis=0)
        at = pos_row - SLOTS * window
        at = jnp.where((at >= 0) & (at < SLOTS), at, -4 * LANES)
        for slot in range(REP):
            if SLOTS * slot < LANES:
                pick = jnp.where(lane == at + SLOTS * slot, 1.0, 0.0).astype(BF)
                values[slot] += jnp.dot(mains, pick, preferred_element_type=F32)
            if SLOTS * (slot + 1) > LANES:
                pick = jnp.where((lane == at + (SLOTS * slot - LANES)) & (lane < LANES // 2), 1.0, 0.0).astype(BF)
                values[slot] += jnp.dot(rests, pick, preferred_element_type=F32)
    for slot in range(REP):
        value = values[slot]
        cycle[pl.ds(slot_owner(place, slot), 16, stride=B), :O] = (value[:16] + value[16:32]) + value[32:]
    b_first = slab_b[0] * B
    b_index = lax.broadcasted_iota(jnp.int32, (B, 1), 0)
    b_label = jnp.zeros((B, 1), jnp.int32)
    b_energy = jnp.zeros((B, 1), F32)
    for b in range(B):
        b_label = jnp.where(b_index == b, vir_irrep[b_first + b], b_label)
        b_energy = jnp.where(b_index == b, vir_energy[b_first + b], b_energy)
    pair_bj = b_label ^ occ
    col_energy = energy_row[...] - b_energy
    for r in range(ROWS):
        row_id = (rep * (FAR * NEAR) + red) * ROWS + r
        a = slab_a[0] * A + row_id // O
        i = row_id % O
        label = vir_irrep[a] ^ occ_irrep[i]
        row_energy = occ_energy[i] - vir_energy[a]
        updated = (cycle[r * B : (r + 1) * B, :O] + other[r]) / (row_energy + col_energy)
        out[r] = jnp.where(pair_bj == label, updated, 0.0)


def own_place():
    return (
        lax.axis_index("far") * NEAR + lax.axis_index("near"),
        lax.axis_index("x") * 2 + lax.axis_index("core"),
    )


SMEM = pl.BlockSpec(memory_space=pltpu.SMEM)
VMEM = pl.BlockSpec(memory_space=pltpu.VMEM)


def params(limit):
    return pltpu.CompilerParams(vmem_limit_bytes=limit * 1024 * 1024)


def call_pack_integrals(place, window, vir_irrep, slab_b, occ_row, integrals):
    return pl.pallas_call(
        functools.partial(pack_integrals, place, window),
        out_shape=(jax.ShapeDtypeStruct((ACROSS, PARTS * BLOCK, LANES), BF), jax.ShapeDtypeStruct((1, 1), jnp.int32)),
        in_specs=[SMEM, SMEM, VMEM, VMEM],
        out_specs=(VMEM, SMEM),
        scratch_shapes=[pltpu.VMEM((ACROSS * PARTS * BLOCK, LANES), F32)],
        compiler_params=params(16),
        cost_estimate=pl.CostEstimate(flops=2 * 10**7, bytes_accessed=600000, transcendentals=0),
        name="pack_integrals",
    )(vir_irrep, slab_b, occ_row, integrals)


def fixed(shape):
    return pl.BlockSpec(shape, lambda step: (0,) * len(shape))


def call_pack_amplitudes(place, window, vir_irrep, occ_irrep, slab_a, occ_row, vir_rows, amplitudes):
    return pl.pallas_call(
        functools.partial(pack_amplitudes, place, window),
        out_shape=jax.ShapeDtypeStruct((TEAM, DEEP * 16, LANES), BF),
        grid=(ROWS // STEP,),
        in_specs=[SMEM, SMEM, SMEM, fixed((1, O)), fixed((1, V)), pl.BlockSpec((STEP, V, O), lambda r: (r, 0, 0))],
        out_specs=fixed((TEAM, DEEP * 16, LANES)),
        scratch_shapes=[
            pltpu.VMEM((16, LANES), jnp.int32),
            pltpu.VMEM((GROUP * LANES, LANES), BF),
            pltpu.VMEM((STEP, V, LANES), F32),
            pltpu.VMEM((ACROSS, V // GROUP // STACK * 16, LANES), F32),
        ],
        compiler_params=params(16),
        cost_estimate=pl.CostEstimate(flops=10**9, bytes_accessed=4500000, transcendentals=0),
        name="pack_amplitudes",
    )(vir_irrep, occ_irrep, slab_a, occ_row, vir_rows, amplitudes)


def call_multiply(place, window, vir_irrep, slab_a, slab_b, occ_row, amps, ints):
    return pl.pallas_call(
        functools.partial(multiply, place, window),
        out_shape=jax.ShapeDtypeStruct((TEAM, 24, LANES), F32),
        in_specs=[SMEM, SMEM, SMEM, VMEM, VMEM] + [VMEM] * 2,
        out_specs=VMEM,
        scratch_shapes=[
            pltpu.VMEM((TEAM * 16, 2 * REP * LANES), BF),
            pltpu.VMEM((2 * REP * LANES, 2 * LANES), BF),
        ],
        compiler_params=params(24),
        name="multiply",
    )(vir_irrep, slab_a, slab_b, occ_row, amps, *ints)


def call_finish(
    place, vir_irrep, occ_irrep, slab_a, slab_b, occ_energy, vir_energy, occ_row, energy_row, other, windows
):
    return pl.pallas_call(
        functools.partial(finish, place),
        out_shape=jax.ShapeDtypeStruct((ROWS, B, O), F32),
        in_specs=[SMEM] * 6 + [VMEM] * (3 + len(windows)),
        out_specs=VMEM,
        scratch_shapes=[pltpu.VMEM((16 * B, LANES), F32)],
        compiler_params=params(16),
        name="finish",
    )(vir_irrep, occ_irrep, slab_a, slab_b, occ_energy, vir_energy, occ_row, energy_row, other, *windows)


def whole_form(amplitudes, integrals, other_terms, occ_energy, vir_energy, occ_irrep, vir_irrep, slab_a, slab_b):
    red, rep = ("far", "near"), ("x", "core")
    red_count = FAR * NEAR
    red_index, rep_index = own_place()
    a_start = slab_a[0] * A
    b_start = slab_b[0] * B
    b_labels = lax.dynamic_slice_in_dim(vir_irrep, b_start, B)
    b_energy = lax.dynamic_slice_in_dim(vir_energy, b_start, B)
    c_labels = lax.dynamic_slice_in_dim(vir_irrep, red_index * ROWS, ROWS)
    pair_ck = pair_labels(c_labels, occ_irrep)
    pair_bj = pair_labels(b_labels, occ_irrep)
    own_pairs = lax.dynamic_slice_in_dim(pair_bj, rep_index, 1, 0)
    local_kept = (pair_ck[:, :, None, None] == own_pairs[None, None]).astype(BF)
    kept = (integrals * local_kept).reshape(1, ROWS * O, O)
    gathered = lax.all_to_all(jnp.broadcast_to(kept, (REP, ROWS * O, O)), rep, 0, 0, tiled=True)
    exchanged = lax.all_to_all(amplitudes, red, split_axis=1, concat_axis=0, tiled=True)
    flat_amps = exchanged.reshape(red_count * ROWS, ROWS * O)
    flat_ints = jnp.swapaxes(gathered, 0, 1).reshape(ROWS * O, B * O)
    parts = jnp.dot(flat_amps, flat_ints, preferred_element_type=F32).reshape(red_count, ROWS, B * O)
    mine = jnp.sum(lax.all_to_all(parts, red, 0, 0, tiled=True), axis=0)
    cycle_term = mine.reshape(ROWS, B, O)
    first_global = (rep_index * red_count + red_index) * ROWS
    row_ids = first_global + jnp.arange(ROWS, dtype=jnp.int32)
    a_index = a_start + row_ids // O
    i_index = row_ids % O
    pair_ai = jnp.bitwise_xor(vir_irrep[a_index], occ_irrep[i_index])
    allowed = pair_ai[:, None, None] == pair_bj[None]
    row_energy = occ_energy[i_index] - vir_energy[a_index]
    col_energy = occ_energy[None, :] - b_energy[:, None]
    denominator = row_energy[:, None, None] + col_energy[None]
    updated = (cycle_term + other_terms) / denominator
    return jnp.where(allowed, updated, jnp.zeros_like(updated))


def packed_form(
    count, amplitudes, integrals, other_terms, occ_energy, vir_energy, occ_irrep, vir_irrep, slab_a, slab_b, ints
):
    occ_row = occ_irrep.reshape(1, O)
    vir_rows = vir_irrep.reshape(1, V)
    windows = [None] * count
    for window in range(count):
        if window > 0:
            ints, _ = call_pack_integrals(
                own_place, window, vir_irrep, slab_b, occ_row, integrals.reshape(ROWS, O, O)
            )
        ints = lax.all_to_all(ints, "x", 0, 0, tiled=True)
        amps = call_pack_amplitudes(own_place, window, vir_irrep, occ_irrep, slab_a, occ_row, vir_rows, amplitudes)
        ints = lax.all_gather(ints, "far", axis=0)
        ints, amps = lax.optimization_barrier((ints, amps))
        both = [ints, lax.ppermute(ints, "core", [(0, 1), (1, 0)])]
        amps = lax.all_to_all(amps, ("near", "x"), 0, 0, tiled=True)
        for col in range(count):
            part = call_multiply(own_place, col, vir_irrep, slab_a, slab_b, occ_row, amps, both)
            windows[col] = part if windows[col] is None else windows[col] + part
    windows = [lax.all_to_all(part, ("near", "x"), 0, 0, tiled=True) for part in windows]
    return call_finish(
        own_place, vir_irrep, occ_irrep, slab_a, slab_b, occ_energy, vir_energy,
        occ_row, occ_energy.reshape(1, O), other_terms, windows,
    )


def on_device(
    amplitudes, integrals, other_terms, occ_energy, vir_energy, occ_irrep, vir_irrep, slab_a, slab_b
):
    args = (amplitudes, integrals, other_terms, occ_energy, vir_energy, occ_irrep, vir_irrep, slab_a, slab_b)
    ints, most = call_pack_integrals(
        own_place, 0, vir_irrep, slab_b, occ_irrep.reshape(1, O), integrals.reshape(ROWS, O, O)
    )

    def crowded(*rest):
        return lax.cond(
            most[0, 0] >= 2 * SLOTS,
            lambda *last: whole_form(*last[:-1]),
            functools.partial(packed_form, 2),
            *rest,
        )

    return lax.cond(most[0, 0] >= SLOTS, crowded, functools.partial(packed_form, 1), *args, ints)


def solution(mesh):
    split = Mesh(mesh.devices.reshape(FAR, NEAR, ACROSS, 2), ("far", "near", "x", "core"))
    rows = P(("x", "core", "far", "near"), None, None)
    placed = (
        rows,
        P(("far", "near"), None, ("x", "core"), None),
        rows,
        P(),
        P(),
        P(),
        P(),
        P(),
        P(),
    )
    return jax.shard_map(
        on_device,
        mesh=split,
        in_specs=placed,
        out_specs=rows,
        check_vma=False,
    )
```

```python
import functools

import jax
import jax.numpy as jnp
from jax import lax
from jax.experimental import pallas as pl
from jax.experimental.pallas import tpu as pltpu
from jax.sharding import Mesh, PartitionSpec as P

A = 64
B = 8
O = 120
V = 960
ROWS = 15
SLOTS = 24
GROUP = 5
PARTS = ROWS // GROUP
STEP = 5
FAR = 8
NEAR = 8
ACROSS = 4
SHARE = SLOTS // ACROSS
TEAM = NEAR * ACROSS
BLOCK = 32
STACK = 4
TWICE = FAR // STACK
DEEP = TWICE * PARTS
REP = 8
LANES = 128
BF = jnp.bfloat16
F32 = jnp.float32


def pair_labels(left, right):
    return jnp.bitwise_xor(left[:, None], right[None, :])


def column_of(row):
    n = row.shape[1]
    same = lax.broadcasted_iota(jnp.int32, (n, n), 0) == lax.broadcasted_iota(jnp.int32, (n, n), 1)
    return jnp.sum(jnp.where(same, row.astype(F32), 0.0), axis=1, keepdims=True).astype(jnp.int32)


def positions(occ_row):
    n = occ_row.shape[1]
    occ_col = column_of(occ_row)
    k_col = lax.broadcasted_iota(jnp.int32, (n, n), 0)
    k_row = lax.broadcasted_iota(jnp.int32, (n, n), 1)
    same = occ_col == occ_row
    row = jnp.sum(jnp.where(same & (k_col < k_row), 1.0, 0.0), axis=0, keepdims=True)
    col = jnp.sum(jnp.where(same & (k_row < k_col), 1.0, 0.0), axis=1, keepdims=True)
    return occ_col, row.astype(jnp.int32), col.astype(jnp.int32)


def thirds(x):
    high = x.astype(BF)
    rest = x - high.astype(F32)
    middle = rest.astype(BF)
    low = (rest - middle.astype(F32)).astype(BF)
    return high, middle, low


def pack_integrals(place, window, vir_irrep, slab_b, occ_row, integrals, out, most, scratch):
    red, rep = place()
    occ = occ_row[...]
    occ_col, pos_row, _ = positions(occ)
    most[0, 0] = jnp.max(pos_row)
    slot = lax.broadcasted_iota(jnp.int32, (SLOTS, O), 0)
    pick = jnp.where(slot == pos_row - SLOTS * window, 1.0, 0.0).astype(BF)
    b_label = vir_irrep[slab_b[0] * B + rep]
    scratch[...] = jnp.zeros_like(scratch)
    for c in range(ROWS):
        label = vir_irrep[red * ROWS + c] ^ b_label
        kept = jnp.where((occ_col ^ label) == occ, integrals[c].astype(F32), 0.0).astype(BF)
        slots = jnp.dot(pick, kept, preferred_element_type=F32)
        for x in range(ACROSS):
            first = (x * PARTS + c // GROUP) * BLOCK + SHARE * (c % GROUP)
            scratch[first : first + SHARE, :O] = slots[x * SHARE : (x + 1) * SHARE]
    for x in range(ACROSS):
        out[x] = scratch[x * PARTS * BLOCK : (x + 1) * PARTS * BLOCK].astype(BF)


def pack_amplitudes(
    place, window, vir_irrep, occ_irrep, slab_a, occ_row, vir_rows, amplitudes, out, starts, chosen, row, packed
):
    red, rep = place()
    step = pl.program_id(0)
    occ = occ_row[...]
    groups = V // GROUP // STACK
    part = NEAR * PARTS

    @pl.when(step == 0)
    def _():
        _, _, pos_col = positions(occ)
        pos_col -= SLOTS * window
        lane = lax.broadcasted_iota(jnp.int32, (O, LANES), 1)
        chosen[...] = jnp.zeros_like(chosen)
        at = pos_col
        for x in range(1, ACROSS):
            at += jnp.where(pos_col >= x * SHARE, BLOCK - SHARE, 0)
        for u in range(GROUP):
            hit = (lane == at + SHARE * u) & (pos_col >= 0) & (pos_col < SLOTS)
            chosen[u * LANES : u * LANES + O] = jnp.where(hit, 1.0, 0.0).astype(BF)
        labels = vir_rows[...]
        for g in range(9):
            below = jnp.sum(jnp.where(labels < g, 1.0, 0.0), axis=1, keepdims=True)
            starts[g : g + 1] = jnp.broadcast_to(below.astype(jnp.int32), (1, LANES))
        for x in range(ACROSS):
            packed[x, pl.ds(ROWS, groups, stride=16), :] = jnp.zeros((groups, LANES), F32)
        row[...] = jnp.zeros_like(row)

    c_index = lax.broadcasted_iota(jnp.int16, (V, O), 0)
    for j in range(STEP):
        row_id = (rep * (FAR * NEAR) + red) * ROWS + step * STEP + j
        label = vir_irrep[slab_a[0] * A + row_id // O] ^ occ_irrep[row_id % O]
        partner = occ ^ label
        low = jnp.zeros((1, O), jnp.int32)
        high = jnp.zeros((1, O), jnp.int32)
        for g in range(8):
            low = jnp.where(partner == g, starts[g : g + 1, :O], low)
            high = jnp.where(partner == g, starts[g + 1 : g + 2, :O], high)
        kept = (c_index >= low.astype(jnp.int16)) & (c_index < high.astype(jnp.int16))
        row[j, :, :O] = jnp.where(kept, amplitudes[j], jnp.zeros((), BF)).astype(F32)
    for j in range(STEP):
        left = jnp.concatenate(
            [row[j, pl.ds(u, V // GROUP, stride=GROUP), :].astype(BF) for u in range(GROUP)], axis=1
        )
        total = jnp.dot(left, chosen[...], preferred_element_type=F32)
        blocks = [
            jnp.concatenate([total[(STACK * t + f) * part : (STACK * t + f + 1) * part] for t in range(TWICE)], axis=0)
            for f in range(STACK)
        ]
        place_of = lax.broadcasted_iota(jnp.int32, (1, LANES), 1) // BLOCK
        for x in range(ACROSS):
            tile = blocks[0] if x == 0 else pltpu.roll(blocks[0], (LANES - BLOCK * x), 1)
            for f in range(1, STACK):
                moved = blocks[f] if x == f else pltpu.roll(blocks[f], (LANES + BLOCK * (f - x)) % LANES, 1)
                tile = jnp.where(place_of == f, moved, tile)
            packed[x, pl.ds(step * STEP + j, groups, stride=16), :] = tile

    @pl.when(step == ROWS // STEP - 1)
    def _():
        rows = PARTS * 16
        for e in range(NEAR):
            for x in range(ACROSS):
                for t in range(TWICE):
                    first = (t * NEAR + e) * rows
                    out[ACROSS * e + x, t * rows : (t + 1) * rows] = packed[x, first : first + rows].astype(BF)


def slot_owner(place, slot):
    _, rep = place()
    return slot % ACROSS * 2 + (rep + slot // ACROSS) % 2


def multiply(place, window, vir_irrep, slab_a, slab_b, occ_row, amps, *rest):
    ints, (out, kept, picks) = rest[:2], rest[2:]
    red, rep = place()
    occ = occ_row[...]
    rows = TEAM * 16
    left = jnp.concatenate([amps[:, k * 16 : (k + 1) * 16].reshape(rows, LANES) for k in range(DEEP)], axis=1)
    _, _, pos_col = positions(occ)
    occ_lanes = jnp.concatenate([occ, jnp.full((1, LANES - O), 64, jnp.int32)], axis=1)
    pos_col -= SLOTS * window
    pos_col = jnp.where((pos_col >= 0) & (pos_col < SLOTS), pos_col, -4 * LANES)
    pos_lanes = jnp.concatenate([pos_col, jnp.full((LANES - O, 1), -4 * LANES, jnp.int32)], axis=0)
    row = lax.broadcasted_iota(jnp.int32, (rows, LANES), 0)
    i_index = (row // (16 * ACROSS)) * ROWS + row % 16
    row_label = jnp.zeros((rows, LANES), jnp.int32)
    for g in range(1, 8):
        start = jnp.sum(jnp.where(occ < g, 1.0, 0.0), axis=1, keepdims=True).astype(jnp.int32)
        row_label += jnp.where(i_index >= start, 1, 0)
    a_label = jnp.zeros((rows, LANES), jnp.int32)
    for x in range(ACROSS):
        label = vir_irrep[slab_a[0] * A + (x * 2 + rep % 2) * FAR + red // NEAR]
        a_label = jnp.where((row // 16) % ACROSS == x, label, a_label)
    row_label = row_label ^ a_label
    wanted = row_label ^ occ_lanes
    lane = lax.broadcasted_iota(jnp.int32, (LANES, 2 * LANES), 1)
    for slot in range(REP):
        pick = jnp.where(lane == pos_lanes + SLOTS * slot, 1.0, 0.0).astype(BF)
        for piece in range(2):
            first = (2 * slot + piece) * LANES
            picks[first : first + LANES] = pick
    for pair in range(REP // 2):
        held = ints[pair * 2 // ACROSS]
        across = (pair * 2 % ACROSS, pair * 2 % ACROSS + 1)
        right = jnp.concatenate(
            [
                jnp.concatenate([held[far, x, g * BLOCK : (g + 1) * BLOCK] for x in across], axis=1)
                for t in range(TWICE)
                for g in range(PARTS)
                for far in range(t * STACK, (t + 1) * STACK)
            ],
            axis=0,
        )
        both = jnp.dot(left, right, preferred_element_type=F32)
        for half in range(2):
            slot = 2 * pair + half
            b_label = vir_irrep[slab_b[0] * B + slot_owner(place, slot)]
            part = both[:, half * LANES : (half + 1) * LANES]
            part = jnp.where(wanted == b_label, part, 0.0)
            high = part.astype(BF)
            first = 2 * slot * LANES
            kept[:, first : first + LANES] = high
            kept[:, first + LANES : first + 2 * LANES] = (part - high.astype(F32)).astype(BF)
    total = jnp.dot(kept[...], picks[...], preferred_element_type=F32)
    rest = total[:, LANES:]
    moved = pltpu.roll(rest, LANES // 2, 1)
    for e in range(TEAM):
        out[e, :16] = total[e * 16 : (e + 1) * 16, :LANES]
        out[e, 16:] = rest[e * 16 : e * 16 + 8] + moved[e * 16 + 8 : e * 16 + 16]


def finish(
    place, vir_irrep, occ_irrep, slab_a, slab_b, occ_energy, vir_energy, occ_row, energy_row, other, *rest
):
    windows, (out, cycle) = rest[:-2], rest[-2:]
    red, rep = place()
    occ = occ_row[...]
    _, pos_row, _ = positions(occ)
    lane = lax.broadcasted_iota(jnp.int32, (LANES, O), 0)
    values = [jnp.zeros((48, O), F32) for _ in range(REP)]
    for window, parts in enumerate(windows):
        total = parts[0]
        for s in range(1, TEAM):
            total += parts[s]
        main = total[:16]
        rest = jnp.concatenate([total[16:], pltpu.roll(total[16:], LANES // 2, 1)], axis=0)
        mains = jnp.concatenate(thirds(main), axis=0)
        rests = jnp.concatenate(thirds(rest), axis=0)
        at = pos_row - SLOTS * window
        at = jnp.where((at >= 0) & (at < SLOTS), at, -4 * LANES)
        for slot in range(REP):
            if SLOTS * slot < LANES:
                pick = jnp.where(lane == at + SLOTS * slot, 1.0, 0.0).astype(BF)
                values[slot] += jnp.dot(mains, pick, preferred_element_type=F32)
            if SLOTS * (slot + 1) > LANES:
                pick = jnp.where((lane == at + (SLOTS * slot - LANES)) & (lane < LANES // 2), 1.0, 0.0).astype(BF)
                values[slot] += jnp.dot(rests, pick, preferred_element_type=F32)
    for slot in range(REP):
        value = values[slot]
        cycle[pl.ds(slot_owner(place, slot), 16, stride=B), :O] = (value[:16] + value[16:32]) + value[32:]
    b_first = slab_b[0] * B
    b_index = lax.broadcasted_iota(jnp.int32, (B, 1), 0)
    b_label = jnp.zeros((B, 1), jnp.int32)
    b_energy = jnp.zeros((B, 1), F32)
    for b in range(B):
        b_label = jnp.where(b_index == b, vir_irrep[b_first + b], b_label)
        b_energy = jnp.where(b_index == b, vir_energy[b_first + b], b_energy)
    pair_bj = b_label ^ occ
    col_energy = energy_row[...] - b_energy
    for r in range(ROWS):
        row_id = (rep * (FAR * NEAR) + red) * ROWS + r
        a = slab_a[0] * A + row_id // O
        i = row_id % O
        label = vir_irrep[a] ^ occ_irrep[i]
        row_energy = occ_energy[i] - vir_energy[a]
        updated = (cycle[r * B : (r + 1) * B, :O] + other[r]) / (row_energy + col_energy)
        out[r] = jnp.where(pair_bj == label, updated, 0.0)


def own_place():
    return (
        lax.axis_index("far") * NEAR + lax.axis_index("near"),
        lax.axis_index("x") * 2 + lax.axis_index("core"),
    )


SMEM = pl.BlockSpec(memory_space=pltpu.SMEM)
VMEM = pl.BlockSpec(memory_space=pltpu.VMEM)


def params(limit):
    return pltpu.CompilerParams(vmem_limit_bytes=limit * 1024 * 1024)


def call_pack_integrals(place, window, vir_irrep, slab_b, occ_row, integrals):
    return pl.pallas_call(
        functools.partial(pack_integrals, place, window),
        out_shape=(jax.ShapeDtypeStruct((ACROSS, PARTS * BLOCK, LANES), BF), jax.ShapeDtypeStruct((1, 1), jnp.int32)),
        in_specs=[SMEM, SMEM, VMEM, VMEM],
        out_specs=(VMEM, SMEM),
        scratch_shapes=[pltpu.VMEM((ACROSS * PARTS * BLOCK, LANES), F32)],
        compiler_params=params(16),
        cost_estimate=pl.CostEstimate(flops=2 * 10**7, bytes_accessed=600000, transcendentals=0),
        name="pack_integrals",
    )(vir_irrep, slab_b, occ_row, integrals)


def fixed(shape):
    return pl.BlockSpec(shape, lambda step: (0,) * len(shape))


def call_pack_amplitudes(place, window, vir_irrep, occ_irrep, slab_a, occ_row, vir_rows, amplitudes):
    return pl.pallas_call(
        functools.partial(pack_amplitudes, place, window),
        out_shape=jax.ShapeDtypeStruct((TEAM, DEEP * 16, LANES), BF),
        grid=(ROWS // STEP,),
        in_specs=[SMEM, SMEM, SMEM, fixed((1, O)), fixed((1, V)), pl.BlockSpec((STEP, V, O), lambda r: (r, 0, 0))],
        out_specs=fixed((TEAM, DEEP * 16, LANES)),
        scratch_shapes=[
            pltpu.VMEM((16, LANES), jnp.int32),
            pltpu.VMEM((GROUP * LANES, LANES), BF),
            pltpu.VMEM((STEP, V, LANES), F32),
            pltpu.VMEM((ACROSS, V // GROUP // STACK * 16, LANES), F32),
        ],
        compiler_params=params(16),
        cost_estimate=pl.CostEstimate(flops=10**9, bytes_accessed=4500000, transcendentals=0),
        name="pack_amplitudes",
    )(vir_irrep, occ_irrep, slab_a, occ_row, vir_rows, amplitudes)


def call_multiply(place, window, vir_irrep, slab_a, slab_b, occ_row, amps, ints):
    return pl.pallas_call(
        functools.partial(multiply, place, window),
        out_shape=jax.ShapeDtypeStruct((TEAM, 24, LANES), F32),
        in_specs=[SMEM, SMEM, SMEM, VMEM, VMEM] + [VMEM] * 2,
        out_specs=VMEM,
        scratch_shapes=[
            pltpu.VMEM((TEAM * 16, 2 * REP * LANES), BF),
            pltpu.VMEM((2 * REP * LANES, 2 * LANES), BF),
        ],
        compiler_params=params(24),
        name="multiply",
    )(vir_irrep, slab_a, slab_b, occ_row, amps, *ints)


def call_finish(
    place, vir_irrep, occ_irrep, slab_a, slab_b, occ_energy, vir_energy, occ_row, energy_row, other, windows
):
    return pl.pallas_call(
        functools.partial(finish, place),
        out_shape=jax.ShapeDtypeStruct((ROWS, B, O), F32),
        in_specs=[SMEM] * 6 + [VMEM] * (3 + len(windows)),
        out_specs=VMEM,
        scratch_shapes=[pltpu.VMEM((16 * B, LANES), F32)],
        compiler_params=params(16),
        name="finish",
    )(vir_irrep, occ_irrep, slab_a, slab_b, occ_energy, vir_energy, occ_row, energy_row, other, *windows)


def whole_form(amplitudes, integrals, other_terms, occ_energy, vir_energy, occ_irrep, vir_irrep, slab_a, slab_b):
    red, rep = ("far", "near"), ("x", "core")
    red_count = FAR * NEAR
    red_index, rep_index = own_place()
    a_start = slab_a[0] * A
    b_start = slab_b[0] * B
    b_labels = lax.dynamic_slice_in_dim(vir_irrep, b_start, B)
    b_energy = lax.dynamic_slice_in_dim(vir_energy, b_start, B)
    c_labels = lax.dynamic_slice_in_dim(vir_irrep, red_index * ROWS, ROWS)
    pair_ck = pair_labels(c_labels, occ_irrep)
    pair_bj = pair_labels(b_labels, occ_irrep)
    own_pairs = lax.dynamic_slice_in_dim(pair_bj, rep_index, 1, 0)
    local_kept = (pair_ck[:, :, None, None] == own_pairs[None, None]).astype(BF)
    kept = (integrals * local_kept).reshape(1, ROWS * O, O)
    gathered = lax.all_to_all(jnp.broadcast_to(kept, (REP, ROWS * O, O)), rep, 0, 0, tiled=True)
    exchanged = lax.all_to_all(amplitudes, red, split_axis=1, concat_axis=0, tiled=True)
    flat_amps = exchanged.reshape(red_count * ROWS, ROWS * O)
    flat_ints = jnp.swapaxes(gathered, 0, 1).reshape(ROWS * O, B * O)
    parts = jnp.dot(flat_amps, flat_ints, preferred_element_type=F32).reshape(red_count, ROWS, B * O)
    mine = jnp.sum(lax.all_to_all(parts, red, 0, 0, tiled=True), axis=0)
    cycle_term = mine.reshape(ROWS, B, O)
    first_global = (rep_index * red_count + red_index) * ROWS
    row_ids = first_global + jnp.arange(ROWS, dtype=jnp.int32)
    a_index = a_start + row_ids // O
    i_index = row_ids % O
    pair_ai = jnp.bitwise_xor(vir_irrep[a_index], occ_irrep[i_index])
    allowed = pair_ai[:, None, None] == pair_bj[None]
    row_energy = occ_energy[i_index] - vir_energy[a_index]
    col_energy = occ_energy[None, :] - b_energy[:, None]
    denominator = row_energy[:, None, None] + col_energy[None]
    updated = (cycle_term + other_terms) / denominator
    return jnp.where(allowed, updated, jnp.zeros_like(updated))


def window_sums(
    window, count, amplitudes, integrals, occ_irrep, vir_irrep, slab_a, slab_b
):
    occ_row = occ_irrep.reshape(1, O)
    vir_rows = vir_irrep.reshape(1, V)
    ints, most = call_pack_integrals(
        own_place, window, vir_irrep, slab_b, occ_row, integrals.reshape(ROWS, O, O)
    )
    ints = lax.all_to_all(ints, "x", 0, 0, tiled=True)
    amps = call_pack_amplitudes(own_place, window, vir_irrep, occ_irrep, slab_a, occ_row, vir_rows, amplitudes)
    ints = lax.all_gather(ints, "far", axis=0)
    ints, amps = lax.optimization_barrier((ints, amps))
    both = [ints, lax.ppermute(ints, "core", [(0, 1), (1, 0)])]
    amps = lax.all_to_all(amps, ("near", "x"), 0, 0, tiled=True)
    parts = [call_multiply(own_place, col, vir_irrep, slab_a, slab_b, occ_row, amps, both) for col in range(count)]
    return parts, most


def last_step(other_terms, occ_energy, vir_energy, occ_irrep, vir_irrep, slab_a, slab_b, *windows):
    return call_finish(
        own_place, vir_irrep, occ_irrep, slab_a, slab_b, occ_energy, vir_energy,
        occ_irrep.reshape(1, O), occ_energy.reshape(1, O), other_terms, windows,
    )


def two_windows(amplitudes, integrals, other_terms, occ_energy, vir_energy, occ_irrep, vir_irrep, slab_a, slab_b):
    sums = [
        window_sums(window, 2, amplitudes, integrals, occ_irrep, vir_irrep, slab_a, slab_b)[0] for window in range(2)
    ]
    windows = [lax.all_to_all(one + two, ("near", "x"), 0, 0, tiled=True) for one, two in zip(*sums)]
    return last_step(other_terms, occ_energy, vir_energy, occ_irrep, vir_irrep, slab_a, slab_b, *windows)


def on_device(
    amplitudes, integrals, other_terms, occ_energy, vir_energy, occ_irrep, vir_irrep, slab_a, slab_b
):
    args = (amplitudes, integrals, other_terms, occ_energy, vir_energy, occ_irrep, vir_irrep, slab_a, slab_b)
    (parts,), most = window_sums(0, 1, amplitudes, integrals, occ_irrep, vir_irrep, slab_a, slab_b)
    parts, most = lax.optimization_barrier((parts, most[0, 0]))
    parts = lax.all_to_all(parts, ("near", "x"), 0, 0, tiled=True)

    def crowded(*rest):
        return lax.cond(most >= 2 * SLOTS, whole_form, two_windows, *rest[:-1])

    return lax.cond(most >= SLOTS, crowded, lambda *rest: last_step(*rest[2:]), *args, parts)


def solution(mesh):
    split = Mesh(mesh.devices.reshape(FAR, NEAR, ACROSS, 2), ("far", "near", "x", "core"))
    rows = P(("x", "core", "far", "near"), None, None)
    placed = (
        rows,
        P(("far", "near"), None, ("x", "core"), None),
        rows,
        P(),
        P(),
        P(),
        P(),
        P(),
        P(),
    )
    return jax.shard_map(
        on_device,
        mesh=split,
        in_specs=placed,
        out_specs=rows,
        check_vma=False,
    )
```

```python
import functools

import jax
import jax.numpy as jnp
from jax import lax
from jax.experimental import pallas as pl
from jax.experimental.pallas import tpu as pltpu
from jax.sharding import Mesh, PartitionSpec as P

A = 64
B = 8
O = 120
V = 960
ROWS = 15
SLOTS = 24
GROUP = 5
PARTS = ROWS // GROUP
STEP = 5
FAR = 8
NEAR = 8
ACROSS = 4
SHARE = SLOTS // ACROSS
TEAM = NEAR * ACROSS
BLOCK = 32
STACK = 4
TWICE = FAR // STACK
DEEP = TWICE * PARTS
REP = 8
LANES = 128
BF = jnp.bfloat16
F32 = jnp.float32


def pair_labels(left, right):
    return jnp.bitwise_xor(left[:, None], right[None, :])


def column_of(row):
    n = row.shape[1]
    same = lax.broadcasted_iota(jnp.int32, (n, n), 0) == lax.broadcasted_iota(jnp.int32, (n, n), 1)
    return jnp.sum(jnp.where(same, row.astype(F32), 0.0), axis=1, keepdims=True).astype(jnp.int32)


def positions(occ_row):
    n = occ_row.shape[1]
    occ_col = column_of(occ_row)
    k_col = lax.broadcasted_iota(jnp.int32, (n, n), 0)
    k_row = lax.broadcasted_iota(jnp.int32, (n, n), 1)
    same = occ_col == occ_row
    row = jnp.sum(jnp.where(same & (k_col < k_row), 1.0, 0.0), axis=0, keepdims=True)
    col = jnp.sum(jnp.where(same & (k_row < k_col), 1.0, 0.0), axis=1, keepdims=True)
    return occ_col, row.astype(jnp.int32), col.astype(jnp.int32)


def thirds(x):
    high = x.astype(BF)
    rest = x - high.astype(F32)
    middle = rest.astype(BF)
    low = (rest - middle.astype(F32)).astype(BF)
    return high, middle, low


def pack_integrals(place, window, vir_irrep, slab_b, occ_row, integrals, out, most, scratch):
    red, rep = place()
    occ = occ_row[...]
    occ_col, pos_row, _ = positions(occ)
    most[0, 0] = jnp.max(pos_row)
    slot = lax.broadcasted_iota(jnp.int32, (SLOTS, O), 0)
    pick = jnp.where(slot == pos_row - SLOTS * window, 1.0, 0.0).astype(BF)
    b_label = vir_irrep[slab_b[0] * B + rep]
    scratch[...] = jnp.zeros_like(scratch)
    for c in range(ROWS):
        label = vir_irrep[red * ROWS + c] ^ b_label
        kept = jnp.where((occ_col ^ label) == occ, integrals[c].astype(F32), 0.0).astype(BF)
        slots = jnp.dot(pick, kept, preferred_element_type=F32)
        for x in range(ACROSS):
            first = (x * PARTS + c // GROUP) * BLOCK + SHARE * (c % GROUP)
            scratch[first : first + SHARE, :O] = slots[x * SHARE : (x + 1) * SHARE]
    for x in range(ACROSS):
        out[x] = scratch[x * PARTS * BLOCK : (x + 1) * PARTS * BLOCK].astype(BF)


def pack_amplitudes(
    place, window, vir_irrep, occ_irrep, slab_a, occ_row, vir_rows, amplitudes, out, starts, chosen, row, packed
):
    red, rep = place()
    step = pl.program_id(0)
    occ = occ_row[...]
    groups = V // GROUP // STACK
    part = NEAR * PARTS

    @pl.when(step == 0)
    def _():
        _, _, pos_col = positions(occ)
        pos_col -= SLOTS * window
        lane = lax.broadcasted_iota(jnp.int32, (O, LANES), 1)
        at = pos_col
        for x in range(1, ACROSS):
            at += jnp.where(pos_col >= x * SHARE, BLOCK - SHARE, 0)
        for u in range(GROUP):
            hit = (lane == at + SHARE * u) & (pos_col >= 0) & (pos_col < SLOTS)
            hit = jnp.concatenate([jnp.where(hit, 1.0, 0.0), jnp.zeros((LANES - O, LANES), F32)], axis=0)
            chosen[u * LANES : (u + 1) * LANES] = hit.astype(BF)
        labels = vir_rows[...]
        for g in range(9):
            below = jnp.sum(jnp.where(labels < g, 1.0, 0.0), axis=1, keepdims=True)
            starts[g : g + 1] = jnp.broadcast_to(below.astype(jnp.int32), (1, LANES))
        for x in range(ACROSS):
            packed[x, pl.ds(ROWS, groups, stride=16), :] = jnp.zeros((groups, LANES), F32)
        row[...] = jnp.zeros_like(row)

    c_index = lax.broadcasted_iota(jnp.int16, (V, O), 0)
    for j in range(STEP):
        row_id = (rep * (FAR * NEAR) + red) * ROWS + step * STEP + j
        label = vir_irrep[slab_a[0] * A + row_id // O] ^ occ_irrep[row_id % O]
        partner = occ ^ label
        low = jnp.zeros((1, O), jnp.int32)
        high = jnp.zeros((1, O), jnp.int32)
        for g in range(8):
            low = jnp.where(partner == g, starts[g : g + 1, :O], low)
            high = jnp.where(partner == g, starts[g + 1 : g + 2, :O], high)
        kept = (c_index >= low.astype(jnp.int16)) & (c_index < high.astype(jnp.int16))
        row[j, :V, :O] = jnp.where(kept, amplitudes[j], jnp.zeros((), BF)).astype(F32)
    for j in range(STEP):
        left = jnp.concatenate(
            [row[j, pl.ds(u, V // GROUP, stride=GROUP), :].astype(BF) for u in range(GROUP)], axis=1
        )
        total = jnp.dot(left, chosen[...], preferred_element_type=F32)
        blocks = [
            jnp.concatenate([total[(STACK * t + f) * part : (STACK * t + f + 1) * part] for t in range(TWICE)], axis=0)
            for f in range(STACK)
        ]
        place_of = lax.broadcasted_iota(jnp.int32, (1, LANES), 1) // BLOCK
        for x in range(ACROSS):
            tile = blocks[0] if x == 0 else pltpu.roll(blocks[0], (LANES - BLOCK * x), 1)
            for f in range(1, STACK):
                moved = blocks[f] if x == f else pltpu.roll(blocks[f], (LANES + BLOCK * (f - x)) % LANES, 1)
                tile = jnp.where(place_of == f, moved, tile)
            packed[x, pl.ds(step * STEP + j, groups, stride=16), :] = tile

    @pl.when(step == ROWS // STEP - 1)
    def _():
        rows = PARTS * 16
        for e in range(NEAR):
            for x in range(ACROSS):
                for t in range(TWICE):
                    first = (t * NEAR + e) * rows
                    out[ACROSS * e + x, t * rows : (t + 1) * rows] = packed[x, first : first + rows].astype(BF)


def slot_owner(place, slot):
    _, rep = place()
    return slot % ACROSS * 2 + (rep + slot // ACROSS) % 2


def multiply(place, window, vir_irrep, slab_a, slab_b, occ_row, amps, *rest):
    ints, (out, kept, picks) = rest[:2], rest[2:]
    red, rep = place()
    occ = occ_row[...]
    rows = TEAM * 16
    left = jnp.concatenate([amps[:, k * 16 : (k + 1) * 16].reshape(rows, LANES) for k in range(DEEP)], axis=1)
    _, _, pos_col = positions(occ)
    occ_lanes = jnp.concatenate([occ, jnp.full((1, LANES - O), 64, jnp.int32)], axis=1)
    pos_col -= SLOTS * window
    pos_col = jnp.where((pos_col >= 0) & (pos_col < SLOTS), pos_col, -4 * LANES)
    pos_lanes = jnp.concatenate([pos_col, jnp.full((LANES - O, 1), -4 * LANES, jnp.int32)], axis=0)
    row = lax.broadcasted_iota(jnp.int32, (rows, LANES), 0)
    i_index = (row // (16 * ACROSS)) * ROWS + row % 16
    row_label = jnp.zeros((rows, LANES), jnp.int32)
    for g in range(1, 8):
        start = jnp.sum(jnp.where(occ < g, 1.0, 0.0), axis=1, keepdims=True).astype(jnp.int32)
        row_label += jnp.where(i_index >= start, 1, 0)
    a_label = jnp.zeros((rows, LANES), jnp.int32)
    for x in range(ACROSS):
        label = vir_irrep[slab_a[0] * A + (x * 2 + rep % 2) * FAR + red // NEAR]
        a_label = jnp.where((row // 16) % ACROSS == x, label, a_label)
    row_label = row_label ^ a_label
    wanted = row_label ^ occ_lanes
    lane = lax.broadcasted_iota(jnp.int32, (LANES, 2 * LANES), 1)
    for slot in range(REP):
        pick = jnp.where(lane == pos_lanes + SLOTS * slot, 1.0, 0.0).astype(BF)
        for piece in range(2):
            first = (2 * slot + piece) * LANES
            picks[first : first + LANES] = pick
    for pair in range(REP // 2):
        held = ints[pair * 2 // ACROSS]
        across = (pair * 2 % ACROSS, pair * 2 % ACROSS + 1)
        right = jnp.concatenate(
            [
                jnp.concatenate([held[far, x, g * BLOCK : (g + 1) * BLOCK] for x in across], axis=1)
                for t in range(TWICE)
                for g in range(PARTS)
                for far in range(t * STACK, (t + 1) * STACK)
            ],
            axis=0,
        )
        both = jnp.dot(left, right, preferred_element_type=F32)
        for half in range(2):
            slot = 2 * pair + half
            b_label = vir_irrep[slab_b[0] * B + slot_owner(place, slot)]
            part = both[:, half * LANES : (half + 1) * LANES]
            part = jnp.where(wanted == b_label, part, 0.0)
            high = part.astype(BF)
            first = 2 * slot * LANES
            kept[:, first : first + LANES] = high
            kept[:, first + LANES : first + 2 * LANES] = (part - high.astype(F32)).astype(BF)
    total = jnp.dot(kept[...], picks[...], preferred_element_type=F32)
    rest = total[:, LANES:]
    moved = pltpu.roll(rest, LANES // 2, 1)
    for e in range(TEAM):
        out[e, :16] = total[e * 16 : (e + 1) * 16, :LANES]
        out[e, 16:] = rest[e * 16 : e * 16 + 8] + moved[e * 16 + 8 : e * 16 + 16]


def finish(
    place, vir_irrep, occ_irrep, slab_a, slab_b, occ_energy, vir_energy, occ_row, energy_row, other, *rest
):
    windows, (out, cycle) = rest[:-2], rest[-2:]
    red, rep = place()
    occ = occ_row[...]
    _, pos_row, _ = positions(occ)
    lane = lax.broadcasted_iota(jnp.int32, (LANES, O), 0)
    values = [jnp.zeros((48, O), F32) for _ in range(REP)]
    for window, parts in enumerate(windows):
        total = parts[0]
        for s in range(1, TEAM):
            total += parts[s]
        main = total[:16]
        rest = jnp.concatenate([total[16:], pltpu.roll(total[16:], LANES // 2, 1)], axis=0)
        mains = jnp.concatenate(thirds(main), axis=0)
        rests = jnp.concatenate(thirds(rest), axis=0)
        at = pos_row - SLOTS * window
        at = jnp.where((at >= 0) & (at < SLOTS), at, -4 * LANES)
        for slot in range(REP):
            if SLOTS * slot < LANES:
                pick = jnp.where(lane == at + SLOTS * slot, 1.0, 0.0).astype(BF)
                values[slot] += jnp.dot(mains, pick, preferred_element_type=F32)
            if SLOTS * (slot + 1) > LANES:
                pick = jnp.where((lane == at + (SLOTS * slot - LANES)) & (lane < LANES // 2), 1.0, 0.0).astype(BF)
                values[slot] += jnp.dot(rests, pick, preferred_element_type=F32)
    for slot in range(REP):
        value = values[slot]
        cycle[pl.ds(slot_owner(place, slot), 16, stride=B), :O] = (value[:16] + value[16:32]) + value[32:]
    b_first = slab_b[0] * B
    b_index = lax.broadcasted_iota(jnp.int32, (B, 1), 0)
    b_label = jnp.zeros((B, 1), jnp.int32)
    b_energy = jnp.zeros((B, 1), F32)
    for b in range(B):
        b_label = jnp.where(b_index == b, vir_irrep[b_first + b], b_label)
        b_energy = jnp.where(b_index == b, vir_energy[b_first + b], b_energy)
    pair_bj = b_label ^ occ
    col_energy = energy_row[...] - b_energy
    for r in range(ROWS):
        row_id = (rep * (FAR * NEAR) + red) * ROWS + r
        a = slab_a[0] * A + row_id // O
        i = row_id % O
        label = vir_irrep[a] ^ occ_irrep[i]
        row_energy = occ_energy[i] - vir_energy[a]
        updated = (cycle[r * B : (r + 1) * B, :O] + other[r]) / (row_energy + col_energy)
        out[r] = jnp.where(pair_bj == label, updated, 0.0)


def own_place():
    return (
        lax.axis_index("far") * NEAR + lax.axis_index("near"),
        lax.axis_index("x") * 2 + lax.axis_index("core"),
    )


SMEM = pl.BlockSpec(memory_space=pltpu.SMEM)
VMEM = pl.BlockSpec(memory_space=pltpu.VMEM)


def params(limit):
    return pltpu.CompilerParams(vmem_limit_bytes=limit * 1024 * 1024)


def call_pack_integrals(place, window, vir_irrep, slab_b, occ_row, integrals):
    return pl.pallas_call(
        functools.partial(pack_integrals, place, window),
        out_shape=(jax.ShapeDtypeStruct((ACROSS, PARTS * BLOCK, LANES), BF), jax.ShapeDtypeStruct((1, 1), jnp.int32)),
        in_specs=[SMEM, SMEM, VMEM, VMEM],
        out_specs=(VMEM, SMEM),
        scratch_shapes=[pltpu.VMEM((ACROSS * PARTS * BLOCK, LANES), F32)],
        compiler_params=params(16),
        cost_estimate=pl.CostEstimate(flops=2 * 10**7, bytes_accessed=600000, transcendentals=0),
        name="pack_integrals",
    )(vir_irrep, slab_b, occ_row, integrals)


def fixed(shape):
    return pl.BlockSpec(shape, lambda step: (0,) * len(shape))


def call_pack_amplitudes(place, window, vir_irrep, occ_irrep, slab_a, occ_row, vir_rows, amplitudes):
    return pl.pallas_call(
        functools.partial(pack_amplitudes, place, window),
        out_shape=jax.ShapeDtypeStruct((TEAM, DEEP * 16, LANES), BF),
        grid=(ROWS // STEP,),
        in_specs=[SMEM, SMEM, SMEM, fixed((1, O)), fixed((1, V)), pl.BlockSpec((STEP, V, O), lambda r: (r, 0, 0))],
        out_specs=fixed((TEAM, DEEP * 16, LANES)),
        scratch_shapes=[
            pltpu.VMEM((16, LANES), jnp.int32),
            pltpu.VMEM((GROUP * LANES, LANES), BF),
            pltpu.VMEM((STEP, V + 8, LANES), F32),
            pltpu.VMEM((ACROSS, V // GROUP // STACK * 16 + 16, LANES), F32),
        ],
        compiler_params=params(16),
        cost_estimate=pl.CostEstimate(flops=10**9, bytes_accessed=4500000, transcendentals=0),
        name="pack_amplitudes",
    )(vir_irrep, occ_irrep, slab_a, occ_row, vir_rows, amplitudes)


def call_multiply(place, window, vir_irrep, slab_a, slab_b, occ_row, amps, ints):
    return pl.pallas_call(
        functools.partial(multiply, place, window),
        out_shape=jax.ShapeDtypeStruct((TEAM, 24, LANES), F32),
        in_specs=[SMEM, SMEM, SMEM, VMEM, VMEM] + [VMEM] * 2,
        out_specs=VMEM,
        scratch_shapes=[
            pltpu.VMEM((TEAM * 16, 2 * REP * LANES), BF),
            pltpu.VMEM((2 * REP * LANES, 2 * LANES), BF),
        ],
        compiler_params=params(24),
        name="multiply",
    )(vir_irrep, slab_a, slab_b, occ_row, amps, *ints)


def call_finish(
    place, vir_irrep, occ_irrep, slab_a, slab_b, occ_energy, vir_energy, occ_row, energy_row, other, windows
):
    return pl.pallas_call(
        functools.partial(finish, place),
        out_shape=jax.ShapeDtypeStruct((ROWS, B, O), F32),
        in_specs=[SMEM] * 6 + [VMEM] * (3 + len(windows)),
        out_specs=VMEM,
        scratch_shapes=[pltpu.VMEM((16 * B + B, LANES), F32)],
        compiler_params=params(16),
        name="finish",
    )(vir_irrep, occ_irrep, slab_a, slab_b, occ_energy, vir_energy, occ_row, energy_row, other, *windows)


def whole_form(amplitudes, integrals, other_terms, occ_energy, vir_energy, occ_irrep, vir_irrep, slab_a, slab_b):
    red, rep = ("far", "near"), ("x", "core")
    red_count = FAR * NEAR
    red_index, rep_index = own_place()
    a_start = slab_a[0] * A
    b_start = slab_b[0] * B
    b_labels = lax.dynamic_slice_in_dim(vir_irrep, b_start, B)
    b_energy = lax.dynamic_slice_in_dim(vir_energy, b_start, B)
    c_labels = lax.dynamic_slice_in_dim(vir_irrep, red_index * ROWS, ROWS)
    pair_ck = pair_labels(c_labels, occ_irrep)
    pair_bj = pair_labels(b_labels, occ_irrep)
    own_pairs = lax.dynamic_slice_in_dim(pair_bj, rep_index, 1, 0)
    local_kept = (pair_ck[:, :, None, None] == own_pairs[None, None]).astype(BF)
    kept = (integrals * local_kept).reshape(1, ROWS * O, O)
    gathered = lax.all_to_all(jnp.broadcast_to(kept, (REP, ROWS * O, O)), rep, 0, 0, tiled=True)
    exchanged = lax.all_to_all(amplitudes, red, split_axis=1, concat_axis=0, tiled=True)
    flat_amps = exchanged.reshape(red_count * ROWS, ROWS * O)
    flat_ints = jnp.swapaxes(gathered, 0, 1).reshape(ROWS * O, B * O)
    parts = jnp.dot(flat_amps, flat_ints, preferred_element_type=F32).reshape(red_count, ROWS, B * O)
    mine = jnp.sum(lax.all_to_all(parts, red, 0, 0, tiled=True), axis=0)
    cycle_term = mine.reshape(ROWS, B, O)
    first_global = (rep_index * red_count + red_index) * ROWS
    row_ids = first_global + jnp.arange(ROWS, dtype=jnp.int32)
    a_index = a_start + row_ids // O
    i_index = row_ids % O
    pair_ai = jnp.bitwise_xor(vir_irrep[a_index], occ_irrep[i_index])
    allowed = pair_ai[:, None, None] == pair_bj[None]
    row_energy = occ_energy[i_index] - vir_energy[a_index]
    col_energy = occ_energy[None, :] - b_energy[:, None]
    denominator = row_energy[:, None, None] + col_energy[None]
    updated = (cycle_term + other_terms) / denominator
    return jnp.where(allowed, updated, jnp.zeros_like(updated))


def window_sums(
    window, count, amplitudes, integrals, occ_irrep, vir_irrep, slab_a, slab_b
):
    occ_row = occ_irrep.reshape(1, O)
    vir_rows = vir_irrep.reshape(1, V)
    ints, most = call_pack_integrals(
        own_place, window, vir_irrep, slab_b, occ_row, integrals.reshape(ROWS, O, O)
    )
    ints = lax.all_to_all(ints, "x", 0, 0, tiled=True)
    amps = call_pack_amplitudes(own_place, window, vir_irrep, occ_irrep, slab_a, occ_row, vir_rows, amplitudes)
    ints = lax.all_gather(ints, "far", axis=0)
    ints, amps = lax.optimization_barrier((ints, amps))
    both = [ints, lax.ppermute(ints, "core", [(0, 1), (1, 0)])]
    amps = lax.all_to_all(amps, ("near", "x"), 0, 0, tiled=True)
    parts = [call_multiply(own_place, col, vir_irrep, slab_a, slab_b, occ_row, amps, both) for col in range(count)]
    return parts, most


def last_step(other_terms, occ_energy, vir_energy, occ_irrep, vir_irrep, slab_a, slab_b, *windows):
    return call_finish(
        own_place, vir_irrep, occ_irrep, slab_a, slab_b, occ_energy, vir_energy,
        occ_irrep.reshape(1, O), occ_energy.reshape(1, O), other_terms, windows,
    )


def two_windows(amplitudes, integrals, other_terms, occ_energy, vir_energy, occ_irrep, vir_irrep, slab_a, slab_b):
    sums = [
        window_sums(window, 2, amplitudes, integrals, occ_irrep, vir_irrep, slab_a, slab_b)[0] for window in range(2)
    ]
    windows = [lax.all_to_all(one + two, ("near", "x"), 0, 0, tiled=True) for one, two in zip(*sums)]
    return last_step(other_terms, occ_energy, vir_energy, occ_irrep, vir_irrep, slab_a, slab_b, *windows)


def on_device(
    amplitudes, integrals, other_terms, occ_energy, vir_energy, occ_irrep, vir_irrep, slab_a, slab_b
):
    args = (amplitudes, integrals, other_terms, occ_energy, vir_energy, occ_irrep, vir_irrep, slab_a, slab_b)
    (parts,), most = window_sums(0, 1, amplitudes, integrals, occ_irrep, vir_irrep, slab_a, slab_b)
    parts, most = lax.optimization_barrier((parts, most[0, 0]))
    parts = lax.all_to_all(parts, ("near", "x"), 0, 0, tiled=True)

    def crowded(*rest):
        return lax.cond(most >= 2 * SLOTS, whole_form, two_windows, *rest[:-1])

    return lax.cond(most >= SLOTS, crowded, lambda *rest: last_step(*rest[2:]), *args, parts)


def solution(mesh):
    split = Mesh(mesh.devices.reshape(FAR, NEAR, ACROSS, 2), ("far", "near", "x", "core"))
    rows = P(("x", "core", "far", "near"), None, None)
    placed = (
        rows,
        P(("far", "near"), None, ("x", "core"), None),
        rows,
        P(),
        P(),
        P(),
        P(),
        P(),
        P(),
    )
    return jax.shard_map(
        on_device,
        mesh=split,
        in_specs=placed,
        out_specs=rows,
        check_vma=False,
    )
```

```python
import functools

import jax
import jax.numpy as jnp
from jax import lax
from jax.experimental import pallas as pl
from jax.experimental.pallas import tpu as pltpu
from jax.sharding import Mesh, PartitionSpec as P

A = 64
B = 8
O = 120
V = 960
ROWS = 15
SLOTS = 24
GROUP = 5
PARTS = ROWS // GROUP
STEP = 5
FAR = 8
NEAR = 8
ACROSS = 4
SHARE = SLOTS // ACROSS
TEAM = NEAR * ACROSS
BLOCK = 32
STACK = 4
TWICE = FAR // STACK
DEEP = TWICE * PARTS
REP = 8
LANES = 128
BF = jnp.bfloat16
F32 = jnp.float32


def pair_labels(left, right):
    return jnp.bitwise_xor(left[:, None], right[None, :])


def column_of(row):
    n = row.shape[1]
    same = lax.broadcasted_iota(jnp.int32, (n, n), 0) == lax.broadcasted_iota(jnp.int32, (n, n), 1)
    return jnp.sum(jnp.where(same, row.astype(F32), 0.0), axis=1, keepdims=True).astype(jnp.int32)


def positions(occ_row):
    n = occ_row.shape[1]
    occ_col = column_of(occ_row)
    k_col = lax.broadcasted_iota(jnp.int32, (n, n), 0)
    k_row = lax.broadcasted_iota(jnp.int32, (n, n), 1)
    same = occ_col == occ_row
    row = jnp.sum(jnp.where(same & (k_col < k_row), 1.0, 0.0), axis=0, keepdims=True)
    col = jnp.sum(jnp.where(same & (k_row < k_col), 1.0, 0.0), axis=1, keepdims=True)
    return occ_col, row.astype(jnp.int32), col.astype(jnp.int32)


def thirds(x):
    high = x.astype(BF)
    rest = x - high.astype(F32)
    middle = rest.astype(BF)
    low = (rest - middle.astype(F32)).astype(BF)
    return high, middle, low


def pack_integrals(place, window, vir_irrep, slab_b, occ_row, integrals, out, most, scratch):
    red, rep = place()
    occ = occ_row[...]
    occ_col, pos_row, _ = positions(occ)
    most[0, 0] = jnp.max(pos_row)
    slot = lax.broadcasted_iota(jnp.int32, (SLOTS, O), 0)
    pick = jnp.where(slot == pos_row - SLOTS * window, 1.0, 0.0).astype(BF)
    b_label = vir_irrep[slab_b[0] * B + rep]
    scratch[...] = jnp.zeros_like(scratch)
    for c in range(ROWS):
        label = vir_irrep[red * ROWS + c] ^ b_label
        kept = jnp.where((occ_col ^ label) == occ, integrals[c].astype(F32), 0.0).astype(BF)
        slots = jnp.dot(pick, kept, preferred_element_type=F32)
        for x in range(ACROSS):
            first = (x * PARTS + c // GROUP) * BLOCK + SHARE * (c % GROUP)
            scratch[first : first + SHARE, :O] = slots[x * SHARE : (x + 1) * SHARE]
    for x in range(ACROSS):
        out[x] = scratch[x * PARTS * BLOCK : (x + 1) * PARTS * BLOCK].astype(BF)


def pack_amplitudes(
    place, window, vir_irrep, occ_irrep, slab_a, occ_row, vir_rows, first_half, second_half, out, starts, chosen, row, packed
):
    red, rep = place()
    step = pl.program_id(0)
    occ = occ_row[...]
    groups = V // GROUP // STACK
    part = NEAR * PARTS

    @pl.when(step == 0)
    def _():
        _, _, pos_col = positions(occ)
        pos_col -= SLOTS * window
        lane = lax.broadcasted_iota(jnp.int32, (O, LANES), 1)
        at = pos_col
        for x in range(1, ACROSS):
            at += jnp.where(pos_col >= x * SHARE, BLOCK - SHARE, 0)
        for u in range(GROUP):
            hit = (lane == at + SHARE * u) & (pos_col >= 0) & (pos_col < SLOTS)
            hit = jnp.concatenate([jnp.where(hit, 1.0, 0.0), jnp.zeros((LANES - O, LANES), F32)], axis=0)
            chosen[u * LANES : (u + 1) * LANES] = hit.astype(BF)
        labels = vir_rows[...]
        for g in range(9):
            below = jnp.sum(jnp.where(labels < g, 1.0, 0.0), axis=1, keepdims=True)
            starts[g : g + 1] = jnp.broadcast_to(below.astype(jnp.int32), (1, LANES))
        for x in range(ACROSS):
            packed[x, pl.ds(ROWS, groups, stride=16), :] = jnp.zeros((groups, LANES), F32)
        row[...] = jnp.zeros_like(row)

    c_index = lax.broadcasted_iota(jnp.int16, (V, O), 0)
    for j in range(STEP):
        row_id = (rep * (FAR * NEAR) + red) * ROWS + step * STEP + j
        label = vir_irrep[slab_a[0] * A + row_id // O] ^ occ_irrep[row_id % O]
        partner = occ ^ label
        low = jnp.zeros((1, O), jnp.int32)
        high = jnp.zeros((1, O), jnp.int32)
        for g in range(8):
            low = jnp.where(partner == g, starts[g : g + 1, :O], low)
            high = jnp.where(partner == g, starts[g + 1 : g + 2, :O], high)
        kept = (c_index >= low.astype(jnp.int16)) & (c_index < high.astype(jnp.int16))
        for half, part_of in enumerate((first_half, second_half)):
            at = slice(half * V // 2, (half + 1) * V // 2)
            row[j, at, :O] = jnp.where(kept[at], part_of[j], jnp.zeros((), BF)).astype(F32)
    for j in range(STEP):
        left = jnp.concatenate(
            [row[j, pl.ds(u, V // GROUP, stride=GROUP), :].astype(BF) for u in range(GROUP)], axis=1
        )
        total = jnp.dot(left, chosen[...], preferred_element_type=F32)
        blocks = [
            jnp.concatenate([total[(STACK * t + f) * part : (STACK * t + f + 1) * part] for t in range(TWICE)], axis=0)
            for f in range(STACK)
        ]
        place_of = lax.broadcasted_iota(jnp.int32, (1, LANES), 1) // BLOCK
        for x in range(ACROSS):
            tile = blocks[0] if x == 0 else pltpu.roll(blocks[0], (LANES - BLOCK * x), 1)
            for f in range(1, STACK):
                moved = blocks[f] if x == f else pltpu.roll(blocks[f], (LANES + BLOCK * (f - x)) % LANES, 1)
                tile = jnp.where(place_of == f, moved, tile)
            packed[x, pl.ds(step * STEP + j, groups, stride=16), :] = tile

    @pl.when(step == ROWS // STEP - 1)
    def _():
        rows = PARTS * 16
        for e in range(NEAR):
            for x in range(ACROSS):
                for t in range(TWICE):
                    first = (t * NEAR + e) * rows
                    out[ACROSS * e + x, t * rows : (t + 1) * rows] = packed[x, first : first + rows].astype(BF)


def slot_owner(place, slot):
    _, rep = place()
    return slot % ACROSS * 2 + (rep + slot // ACROSS) % 2


def multiply(place, window, vir_irrep, slab_a, slab_b, occ_row, amps, *rest):
    ints, (out, kept, picks) = rest[:2], rest[2:]
    red, rep = place()
    occ = occ_row[...]
    rows = TEAM * 16
    left = jnp.concatenate([amps[:, k * 16 : (k + 1) * 16].reshape(rows, LANES) for k in range(DEEP)], axis=1)
    _, _, pos_col = positions(occ)
    occ_lanes = jnp.concatenate([occ, jnp.full((1, LANES - O), 64, jnp.int32)], axis=1)
    pos_col -= SLOTS * window
    pos_col = jnp.where((pos_col >= 0) & (pos_col < SLOTS), pos_col, -4 * LANES)
    pos_lanes = jnp.concatenate([pos_col, jnp.full((LANES - O, 1), -4 * LANES, jnp.int32)], axis=0)
    row = lax.broadcasted_iota(jnp.int32, (rows, LANES), 0)
    i_index = (row // (16 * ACROSS)) * ROWS + row % 16
    row_label = jnp.zeros((rows, LANES), jnp.int32)
    for g in range(1, 8):
        start = jnp.sum(jnp.where(occ < g, 1.0, 0.0), axis=1, keepdims=True).astype(jnp.int32)
        row_label += jnp.where(i_index >= start, 1, 0)
    a_label = jnp.zeros((rows, LANES), jnp.int32)
    for x in range(ACROSS):
        label = vir_irrep[slab_a[0] * A + (x * 2 + rep % 2) * FAR + red // NEAR]
        a_label = jnp.where((row // 16) % ACROSS == x, label, a_label)
    row_label = row_label ^ a_label
    wanted = row_label ^ occ_lanes
    lane = lax.broadcasted_iota(jnp.int32, (LANES, 2 * LANES), 1)
    for slot in range(REP):
        pick = jnp.where(lane == pos_lanes + SLOTS * slot, 1.0, 0.0).astype(BF)
        for piece in range(2):
            first = (2 * slot + piece) * LANES
            picks[first : first + LANES] = pick
    for pair in range(REP // 2):
        held = ints[pair * 2 // ACROSS]
        across = (pair * 2 % ACROSS, pair * 2 % ACROSS + 1)
        right = jnp.concatenate(
            [
                jnp.concatenate([held[far, x, g * BLOCK : (g + 1) * BLOCK] for x in across], axis=1)
                for t in range(TWICE)
                for g in range(PARTS)
                for far in range(t * STACK, (t + 1) * STACK)
            ],
            axis=0,
        )
        both = jnp.dot(left, right, preferred_element_type=F32)
        for half in range(2):
            slot = 2 * pair + half
            b_label = vir_irrep[slab_b[0] * B + slot_owner(place, slot)]
            part = both[:, half * LANES : (half + 1) * LANES]
            part = jnp.where(wanted == b_label, part, 0.0)
            high = part.astype(BF)
            first = 2 * slot * LANES
            kept[:, first : first + LANES] = high
            kept[:, first + LANES : first + 2 * LANES] = (part - high.astype(F32)).astype(BF)
    total = jnp.dot(kept[...], picks[...], preferred_element_type=F32)
    rest = total[:, LANES:]
    moved = pltpu.roll(rest, LANES // 2, 1)
    for e in range(TEAM):
        out[e, :16] = total[e * 16 : (e + 1) * 16, :LANES]
        out[e, 16:] = rest[e * 16 : e * 16 + 8] + moved[e * 16 + 8 : e * 16 + 16]


def finish(
    place, vir_irrep, occ_irrep, slab_a, slab_b, occ_energy, vir_energy, occ_row, energy_row, other, *rest
):
    windows, (out, cycle) = rest[:-2], rest[-2:]
    red, rep = place()
    occ = occ_row[...]
    _, pos_row, _ = positions(occ)
    lane = lax.broadcasted_iota(jnp.int32, (LANES, O), 0)
    values = [jnp.zeros((48, O), F32) for _ in range(REP)]
    for window, parts in enumerate(windows):
        total = parts[0]
        for s in range(1, TEAM):
            total += parts[s]
        main = total[:16]
        rest = jnp.concatenate([total[16:], pltpu.roll(total[16:], LANES // 2, 1)], axis=0)
        mains = jnp.concatenate(thirds(main), axis=0)
        rests = jnp.concatenate(thirds(rest), axis=0)
        at = pos_row - SLOTS * window
        at = jnp.where((at >= 0) & (at < SLOTS), at, -4 * LANES)
        for slot in range(REP):
            if SLOTS * slot < LANES:
                pick = jnp.where(lane == at + SLOTS * slot, 1.0, 0.0).astype(BF)
                values[slot] += jnp.dot(mains, pick, preferred_element_type=F32)
            if SLOTS * (slot + 1) > LANES:
                pick = jnp.where((lane == at + (SLOTS * slot - LANES)) & (lane < LANES // 2), 1.0, 0.0).astype(BF)
                values[slot] += jnp.dot(rests, pick, preferred_element_type=F32)
    for slot in range(REP):
        value = values[slot]
        cycle[pl.ds(slot_owner(place, slot), 16, stride=B), :O] = (value[:16] + value[16:32]) + value[32:]
    b_first = slab_b[0] * B
    b_index = lax.broadcasted_iota(jnp.int32, (B, 1), 0)
    b_label = jnp.zeros((B, 1), jnp.int32)
    b_energy = jnp.zeros((B, 1), F32)
    for b in range(B):
        b_label = jnp.where(b_index == b, vir_irrep[b_first + b], b_label)
        b_energy = jnp.where(b_index == b, vir_energy[b_first + b], b_energy)
    pair_bj = b_label ^ occ
    col_energy = energy_row[...] - b_energy
    for r in range(ROWS):
        row_id = (rep * (FAR * NEAR) + red) * ROWS + r
        a = slab_a[0] * A + row_id // O
        i = row_id % O
        label = vir_irrep[a] ^ occ_irrep[i]
        row_energy = occ_energy[i] - vir_energy[a]
        updated = (cycle[r * B : (r + 1) * B, :O] + other[r]) / (row_energy + col_energy)
        out[r] = jnp.where(pair_bj == label, updated, 0.0)


def own_place():
    return (
        lax.axis_index("far") * NEAR + lax.axis_index("near"),
        lax.axis_index("x") * 2 + lax.axis_index("core"),
    )


SMEM = pl.BlockSpec(memory_space=pltpu.SMEM)
VMEM = pl.BlockSpec(memory_space=pltpu.VMEM)


def params(limit):
    return pltpu.CompilerParams(vmem_limit_bytes=limit * 1024 * 1024)


def call_pack_integrals(place, window, vir_irrep, slab_b, occ_row, integrals):
    return pl.pallas_call(
        functools.partial(pack_integrals, place, window),
        out_shape=(jax.ShapeDtypeStruct((ACROSS, PARTS * BLOCK, LANES), BF), jax.ShapeDtypeStruct((1, 1), jnp.int32)),
        in_specs=[SMEM, SMEM, VMEM, VMEM],
        out_specs=(VMEM, SMEM),
        scratch_shapes=[pltpu.VMEM((ACROSS * PARTS * BLOCK, LANES), F32)],
        compiler_params=params(16),
        cost_estimate=pl.CostEstimate(flops=2 * 10**7, bytes_accessed=600000, transcendentals=0),
        name="pack_integrals",
    )(vir_irrep, slab_b, occ_row, integrals)


def fixed(shape):
    return pl.BlockSpec(shape, lambda step: (0,) * len(shape))


def call_pack_amplitudes(place, window, vir_irrep, occ_irrep, slab_a, occ_row, vir_rows, amplitudes):
    return pl.pallas_call(
        functools.partial(pack_amplitudes, place, window),
        out_shape=jax.ShapeDtypeStruct((TEAM, DEEP * 16, LANES), BF),
        grid=(ROWS // STEP,),
        in_specs=[SMEM, SMEM, SMEM, fixed((1, O)), fixed((1, V)), pl.BlockSpec((STEP, V // 2, O), lambda r: (r, 0, 0)), pl.BlockSpec((STEP, V // 2, O), lambda r: (r, 1, 0))],
        out_specs=fixed((TEAM, DEEP * 16, LANES)),
        scratch_shapes=[
            pltpu.VMEM((16, LANES), jnp.int32),
            pltpu.VMEM((GROUP * LANES, LANES), BF),
            pltpu.VMEM((STEP, V + 8, LANES), F32),
            pltpu.VMEM((ACROSS, V // GROUP // STACK * 16 + 16, LANES), F32),
        ],
        compiler_params=params(16),
        cost_estimate=pl.CostEstimate(flops=10**9, bytes_accessed=4500000, transcendentals=0),
        name="pack_amplitudes",
    )(vir_irrep, occ_irrep, slab_a, occ_row, vir_rows, amplitudes, amplitudes)


def call_multiply(place, window, vir_irrep, slab_a, slab_b, occ_row, amps, ints):
    return pl.pallas_call(
        functools.partial(multiply, place, window),
        out_shape=jax.ShapeDtypeStruct((TEAM, 24, LANES), F32),
        in_specs=[SMEM, SMEM, SMEM, VMEM, VMEM] + [VMEM] * 2,
        out_specs=VMEM,
        scratch_shapes=[
            pltpu.VMEM((TEAM * 16, 2 * REP * LANES), BF),
            pltpu.VMEM((2 * REP * LANES, 2 * LANES), BF),
        ],
        compiler_params=params(24),
        name="multiply",
    )(vir_irrep, slab_a, slab_b, occ_row, amps, *ints)


def call_finish(
    place, vir_irrep, occ_irrep, slab_a, slab_b, occ_energy, vir_energy, occ_row, energy_row, other, windows
):
    return pl.pallas_call(
        functools.partial(finish, place),
        out_shape=jax.ShapeDtypeStruct((ROWS, B, O), F32),
        in_specs=[SMEM] * 6 + [VMEM] * (3 + len(windows)),
        out_specs=VMEM,
        scratch_shapes=[pltpu.VMEM((16 * B + B, LANES), F32)],
        compiler_params=params(16),
        name="finish",
    )(vir_irrep, occ_irrep, slab_a, slab_b, occ_energy, vir_energy, occ_row, energy_row, other, *windows)


def whole_form(amplitudes, integrals, other_terms, occ_energy, vir_energy, occ_irrep, vir_irrep, slab_a, slab_b):
    red, rep = ("far", "near"), ("x", "core")
    red_count = FAR * NEAR
    red_index, rep_index = own_place()
    a_start = slab_a[0] * A
    b_start = slab_b[0] * B
    b_labels = lax.dynamic_slice_in_dim(vir_irrep, b_start, B)
    b_energy = lax.dynamic_slice_in_dim(vir_energy, b_start, B)
    c_labels = lax.dynamic_slice_in_dim(vir_irrep, red_index * ROWS, ROWS)
    pair_ck = pair_labels(c_labels, occ_irrep)
    pair_bj = pair_labels(b_labels, occ_irrep)
    own_pairs = lax.dynamic_slice_in_dim(pair_bj, rep_index, 1, 0)
    local_kept = (pair_ck[:, :, None, None] == own_pairs[None, None]).astype(BF)
    kept = (integrals * local_kept).reshape(1, ROWS * O, O)
    gathered = lax.all_to_all(jnp.broadcast_to(kept, (REP, ROWS * O, O)), rep, 0, 0, tiled=True)
    exchanged = lax.all_to_all(amplitudes, red, split_axis=1, concat_axis=0, tiled=True)
    flat_amps = exchanged.reshape(red_count * ROWS, ROWS * O)
    flat_ints = jnp.swapaxes(gathered, 0, 1).reshape(ROWS * O, B * O)
    parts = jnp.dot(flat_amps, flat_ints, preferred_element_type=F32).reshape(red_count, ROWS, B * O)
    mine = jnp.sum(lax.all_to_all(parts, red, 0, 0, tiled=True), axis=0)
    cycle_term = mine.reshape(ROWS, B, O)
    first_global = (rep_index * red_count + red_index) * ROWS
    row_ids = first_global + jnp.arange(ROWS, dtype=jnp.int32)
    a_index = a_start + row_ids // O
    i_index = row_ids % O
    pair_ai = jnp.bitwise_xor(vir_irrep[a_index], occ_irrep[i_index])
    allowed = pair_ai[:, None, None] == pair_bj[None]
    row_energy = occ_energy[i_index] - vir_energy[a_index]
    col_energy = occ_energy[None, :] - b_energy[:, None]
    denominator = row_energy[:, None, None] + col_energy[None]
    updated = (cycle_term + other_terms) / denominator
    return jnp.where(allowed, updated, jnp.zeros_like(updated))


def window_sums(
    window, count, amplitudes, integrals, occ_irrep, vir_irrep, slab_a, slab_b
):
    occ_row = occ_irrep.reshape(1, O)
    vir_rows = vir_irrep.reshape(1, V)
    ints, most = call_pack_integrals(
        own_place, window, vir_irrep, slab_b, occ_row, integrals.reshape(ROWS, O, O)
    )
    ints = lax.all_to_all(ints, "x", 0, 0, tiled=True)
    amps = call_pack_amplitudes(own_place, window, vir_irrep, occ_irrep, slab_a, occ_row, vir_rows, amplitudes)
    ints = lax.all_gather(ints, "far", axis=0)
    ints, amps = lax.optimization_barrier((ints, amps))
    both = [ints, lax.ppermute(ints, "core", [(0, 1), (1, 0)])]
    amps = lax.all_to_all(amps, ("near", "x"), 0, 0, tiled=True)
    parts = [call_multiply(own_place, col, vir_irrep, slab_a, slab_b, occ_row, amps, both) for col in range(count)]
    return parts, most


def last_step(other_terms, occ_energy, vir_energy, occ_irrep, vir_irrep, slab_a, slab_b, *windows):
    return call_finish(
        own_place, vir_irrep, occ_irrep, slab_a, slab_b, occ_energy, vir_energy,
        occ_irrep.reshape(1, O), occ_energy.reshape(1, O), other_terms, windows,
    )


def two_windows(amplitudes, integrals, other_terms, occ_energy, vir_energy, occ_irrep, vir_irrep, slab_a, slab_b):
    sums = [
        window_sums(window, 2, amplitudes, integrals, occ_irrep, vir_irrep, slab_a, slab_b)[0] for window in range(2)
    ]
    windows = [lax.all_to_all(one + two, ("near", "x"), 0, 0, tiled=True) for one, two in zip(*sums)]
    return last_step(other_terms, occ_energy, vir_energy, occ_irrep, vir_irrep, slab_a, slab_b, *windows)


def on_device(
    amplitudes, integrals, other_terms, occ_energy, vir_energy, occ_irrep, vir_irrep, slab_a, slab_b
):
    args = (amplitudes, integrals, other_terms, occ_energy, vir_energy, occ_irrep, vir_irrep, slab_a, slab_b)
    (parts,), most = window_sums(0, 1, amplitudes, integrals, occ_irrep, vir_irrep, slab_a, slab_b)
    parts, most = lax.optimization_barrier((parts, most[0, 0]))
    parts = lax.all_to_all(parts, ("near", "x"), 0, 0, tiled=True)

    def crowded(*rest):
        return lax.cond(most >= 2 * SLOTS, whole_form, two_windows, *rest[:-1])

    return lax.cond(most >= SLOTS, crowded, lambda *rest: last_step(*rest[2:]), *args, parts)


def solution(mesh):
    split = Mesh(mesh.devices.reshape(FAR, NEAR, ACROSS, 2), ("far", "near", "x", "core"))
    rows = P(("x", "core", "far", "near"), None, None)
    placed = (
        rows,
        P(("far", "near"), None, ("x", "core"), None),
        rows,
        P(),
        P(),
        P(),
        P(),
        P(),
        P(),
    )
    return jax.shard_map(
        on_device,
        mesh=split,
        in_specs=placed,
        out_specs=rows,
        check_vma=False,
    )
```
